512 devices in a mesh: dom: 128 (over y, z, core), row: 4 (over x).
Axes of the slice: x: 4, y: 8, z: 8, core: 2. Of those that a mesh axis runs over, the one named last changes fastest.
Arguments:
- features: bfloat16 [65536, 256], P(('dom', 'row')), may hold values from -6 to 6
- history: bfloat16 [65536, 256], P(('dom', 'row')), may hold values from -6 to 6
- inner_adj: bfloat16 [65536, 512], P(('dom', 'row')), as said below
- halo_tiles: bfloat16 [32768, 4096], P(('dom', 'row')), may hold values from -0.125 to 0.125
- tile_target: int32 [512, 1024], P(('dom', 'row')), may hold values from 0 to 1
- pair_counts: int32 [512, 512], P(('dom', 'row')), may hold values from 0 to 2
- send_blocks: int32 [512, 1024], P(('dom', 'row')), may hold values from 0 to 31
- weight1: bfloat16 [256, 256], replicated, may hold values from -0.375 to 0.375
- weight2: bfloat16 [256, 256], replicated, may hold values from -0.375 to 0.375
- out_cotangent: bfloat16 [65536, 256], P(('dom', 'row')), may hold values from -0.0234375 to 0.0234375
Outputs:
- fresh_history: bfloat16 [65536, 256], P(('dom', 'row'))
- layer_out: bfloat16 [65536, 256], P(('dom', 'row'))
- grad_w1: float32 [256, 256], replicated
- grad_w2: float32 [256, 256], replicated
The draws below stay inside these ranges and needn't reach their ends.
Inputs may be any that keep to these rules, and one draw needn't show every extreme that they name: pair_counts[e, o] blocks of the 2 slots from owner o to requester e are used, the lowest slots first; some pair uses all 2. Each partition's 512 x 512 block of inner_adj is symmetric.
All inputs are finite; a program needn't handle non-finite values.
Results may differ from the reference program's by a relative error of at most 0.011.
Values may be sent and summed in bfloat16 or wider, within the bound.
A program may use at most 64 MiB of HBM per device.

```python
import jax
import jax.numpy as jnp
from jax import lax

D = 256
NBL = 128
TB = 64
RB = 4
CAP = 2
HB = 32
NB_P = 512
DEVS = 512
NODES = 65536
SLOTS = 4096
N_DOM = 128
N_ROW = 4


def draw_inner_adj(key, part):
    key = jax.random.fold_in(key, 11)
    groups = NODES // NB_P
    raw = jax.random.normal(key, (groups, NB_P, NB_P), jnp.float32)
    symmetric = (raw + jnp.swapaxes(raw, 1, 2)) * (1.0 / (2.0 * NB_P) ** 0.5)
    return symmetric.reshape(NODES, NB_P).astype(jnp.bfloat16)


def plant(entries, key, low, high):
    place = [jax.random.randint(jax.random.fold_in(key, axis), (), 0, length) for axis, length in enumerate(entries.shape)]
    main_axis = entries.shape.index(max(entries.shape))
    next_to = place[:main_axis] + [(place[main_axis] + 1) % entries.shape[main_axis]] + place[main_axis + 1:]
    return entries.at[tuple(place)].set(low).at[tuple(next_to)].set(high)


def block_scale(key, dims, shards, least, high):
    level = 1.0
    for dim, blocks in shards:
        steps = jax.random.uniform(jax.random.fold_in(jax.random.fold_in(key, 6), dim), (blocks,), jnp.float32, least / len(shards), high / len(shards))
        level = level * jnp.repeat(jnp.exp(steps), dims[dim] // blocks).reshape((-1,) + (1,) * (len(dims) - 1 - dim))
    return level


def gaussian(rng, extent, deviation, most, pieces=(), kind=jnp.bfloat16):
    result = jax.random.normal(rng, extent, jnp.float32) * deviation
    if len(pieces) > 0:
        result = block_scale(rng, extent, pieces, -0.22, 0.18) * result
    return jnp.clip(result, min=-most, max=most).astype(kind)


def setup_inputs(seed: int = 0) -> dict:
    keys = jax.random.split(jax.random.key(seed), 11)
    features = gaussian(keys[0], (NODES, D), 1.0, 6.0, ((0, 512),))
    history = gaussian(keys[1], (NODES, D), 1.0, 6.0, ((0, 512),))
    inner_adj = draw_inner_adj(jax.random.fold_in(keys[10], 71), 0)
    halo_tiles = gaussian(keys[3], (DEVS * TB, SLOTS), (SLOTS * TB // NBL) ** -0.5, 0.125, ((0, 512),))
    tile_target = plant(jax.random.randint(keys[4], (DEVS, DEVS * CAP), 0, NBL // TB), jax.random.fold_in(keys[4], 1), 0, (NBL // TB) - 1).astype(jnp.int32)
    pair_counts = plant(jax.random.randint(keys[5], (DEVS, DEVS), 0, CAP + 1), jax.random.fold_in(keys[5], 1), 0, CAP).astype(jnp.int32)
    send_blocks = plant(jax.random.randint(keys[6], (DEVS, DEVS * CAP), 0, HB), jax.random.fold_in(keys[6], 1), 0, HB - 1).astype(jnp.int32)
    weight1 = gaussian(keys[7], (D, D), D ** -0.5, 0.375)
    weight2 = gaussian(keys[8], (D, D), D ** -0.5, 0.375)
    out_cotangent = gaussian(keys[9], (NODES, D), NODES ** -0.5, 0.0234375, ((0, 512),))
    return {"features": features, "history": history, "inner_adj": inner_adj, "halo_tiles": halo_tiles, "tile_target": tile_target, "pair_counts": pair_counts, "send_blocks": send_blocks, "weight1": weight1, "weight2": weight2, "out_cotangent": out_cotangent}


def silu_slope(value):
    sig = jax.nn.sigmoid(value)
    return sig * (1.0 + value * (1.0 - sig))


def expand_tiles(tiles, targets, counts):
    nblocks = targets.shape[0]
    usable = (jnp.arange(nblocks, dtype=jnp.int32) % CAP) < jnp.repeat(counts, CAP)
    tile_ids = jnp.arange(NBL // TB, dtype=jnp.int32)
    select = ((targets[None, :] == tile_ids[:, None]) & usable[None, :]).astype(jnp.bfloat16)
    select_rows = jnp.repeat(select, RB, axis=1)
    return (select_rows[:, None, :] * tiles[None, :, :]).reshape(NBL, SLOTS)


def halo_rows(source, send_blocks, device):
    picked = lax.dynamic_slice_in_dim(send_blocks, (device * CAP).astype(jnp.int32), CAP, 1)
    owners = jnp.arange(DEVS, dtype=jnp.int32)
    row_ids = owners[:, None, None] * NBL + picked[:, :, None] * RB + jnp.arange(RB, dtype=jnp.int32)[None, None, :]
    return jnp.take(source, row_ids.reshape(-1), axis=0)


def aggregate(inner_src, halo_src, inner_adj, halo_tiles, tile_target, pair_counts, send_blocks):
    def one_device(device):
        adjacency = lax.dynamic_slice_in_dim(inner_adj, (device * NBL).astype(jnp.int32), NBL, 0)
        partition = device // N_ROW
        members = lax.dynamic_slice_in_dim(inner_src, (partition * NB_P).astype(jnp.int32), NB_P, 0)
        tiles = lax.dynamic_slice_in_dim(halo_tiles, (device * TB).astype(jnp.int32), TB, 0)
        expanded = expand_tiles(tiles, tile_target[device], pair_counts[device])
        total = jnp.dot(adjacency, members, preferred_element_type=jnp.float32)
        total = total + jnp.dot(expanded, halo_rows(halo_src, send_blocks, device), preferred_element_type=jnp.float32)
        return total.astype(jnp.bfloat16)

    stacked = lax.map(one_device, jnp.arange(DEVS, dtype=jnp.int32))
    return stacked.reshape(NODES, D)


def reference(features, history, inner_adj, halo_tiles, tile_target, pair_counts, send_blocks, weight1, weight2, out_cotangent):
    mixed_first = aggregate(features, features, inner_adj, halo_tiles, tile_target, pair_counts, send_blocks)
    pre_first = jnp.dot(mixed_first, weight1, preferred_element_type=jnp.float32)
    fresh_history = jax.nn.silu(pre_first).astype(jnp.bfloat16)
    mixed_second = aggregate(fresh_history, history, inner_adj, halo_tiles, tile_target, pair_counts, send_blocks)
    pre_second = jnp.dot(mixed_second, weight2, preferred_element_type=jnp.float32)
    layer_out = jax.nn.silu(pre_second).astype(jnp.bfloat16)
    back_second = (out_cotangent.astype(jnp.float32) * silu_slope(pre_second)).astype(jnp.bfloat16)
    grad_w2 = jnp.dot(mixed_second.T, back_second, preferred_element_type=jnp.float32)
    upstream = jnp.dot(back_second, weight2.T, preferred_element_type=jnp.float32).astype(jnp.bfloat16)

    def one_partition(partition):
        block = lax.dynamic_slice_in_dim(inner_adj, (partition * NB_P).astype(jnp.int32), NB_P, 0)
        grads = lax.dynamic_slice_in_dim(upstream, (partition * NB_P).astype(jnp.int32), NB_P, 0)
        return lax.dot_general(block, grads, (((0,), (0,)), ((), ())), preferred_element_type=jnp.float32)

    spread = lax.map(one_partition, jnp.arange(N_DOM, dtype=jnp.int32)).reshape(NODES, D)
    back_first = (spread * silu_slope(pre_first)).astype(jnp.bfloat16)
    grad_w1 = jnp.dot(mixed_first.T, back_first, preferred_element_type=jnp.float32)
    return fresh_history, layer_out, grad_w1, grad_w2
```

```python
import functools

import jax
import jax.numpy as jnp
from jax import lax
from jax.experimental import pallas as pl
from jax.experimental.pallas import tpu as pltpu
from jax.sharding import PartitionSpec as P

RB = 4
CAP = 2
NY = 8
NZ = 8
NC = 2
NX = 4
ROWS = 128
WIDTH = 256
MESH = pl.DeviceIdType.MESH


def sigmoid(value):
    return 1.0 / (1.0 + jnp.exp(-value))


def silu_slope(value):
    sig = sigmoid(value)
    return sig * (1.0 + value * (1.0 - sig))


def dot(left, right, dims=((1,), (0,))):
    return lax.dot_general(left, right, (dims, ((), ())), preferred_element_type=jnp.float32)


def expand_tiles(halo_tiles, targets, counts, node_rows):
    nblocks = targets.shape[0]
    slot_rows = halo_tiles.shape[1]
    block_rows = slot_rows // nblocks
    usable = jnp.arange(nblocks, dtype=jnp.int32) % CAP < jnp.repeat(counts, CAP)
    tile_ids = jnp.arange(node_rows // halo_tiles.shape[0], dtype=jnp.int32)
    select = ((targets[None, :] == tile_ids[:, None]) & usable[None, :]).astype(jnp.bfloat16)
    select_rows = jnp.repeat(select, block_rows, axis=1)
    return (select_rows[:, None, :] * halo_tiles[None, :, :]).reshape(node_rows, slot_rows)


def pick_blocks(source, send_blocks, n_dom, n_row):
    width = source.shape[1]
    blocked = source.reshape(-1, RB, width)
    picked = jnp.take(blocked, send_blocks[0], axis=0)
    return picked.reshape(n_dom, n_row, CAP * RB, width)


def position():
    dom = lax.axis_index("dom")
    return dom // (NZ * NC), (dom // NC) % NZ, dom % NC, lax.axis_index("row")


def device(y, z, c, x):
    return ((y * NZ + z) * NC + c, x)


class Links:
    def __init__(self, send, recv):
        self.send, self.recv, self.used = send, recv, 0

    def copy(self, src, dst, target):
        made = pltpu.make_async_remote_copy(
            src_ref=src,
            dst_ref=dst,
            send_sem=self.send.at[self.used],
            recv_sem=self.recv.at[self.used],
            device_id=target,
            device_id_type=MESH,
        )
        self.used += 1
        made.start()
        return made


def tail_kernel(
    feat, halo1, halo2, adj, w1, w2, cot,
    fresh_out, layer_out, grad1, grad2,
    rows, share, half, from_core, from_x, part_x, from_z, part_z, from_y, whole_z, whole_x, send, recv,
):
    y, z, c, x = position()
    links = Links(send, recv)
    peers = [device(y, z, c, (x + k) % NX) for k in range(1, NX)]
    peers += [device(y, (z + k) % NZ, c, x) for k in range(1, NZ)]
    peers += [device((y + k) % NY, z, c, x) for k in range(1, NY)]
    peers += [device(y, z, 1 - c, x)]
    barrier = pltpu.get_barrier_semaphore()
    for peer in peers:
        pl.semaphore_signal(barrier, inc=1, device_id=peer, device_id_type=MESH)
    pl.semaphore_wait(barrier, len(peers))
    x_peers, z_peers, y_peers, twin = peers[:3], peers[3:10], peers[10:17], peers[17]
    mine = pl.ds(pl.multiple_of(x * ROWS, ROWS), ROWS)

    def spread_rows(slot, value):
        rows[slot, mine, :] = value
        return [links.copy(rows.at[slot, mine, :], rows.at[slot, mine, :], peer) for peer in x_peers]

    def finish(copies):
        for copy in copies:
            copy.wait()

    copies = spread_rows(0, feat[...])
    finish(copies)
    mixed1 = (dot(adj[...], rows[0]) + halo1[...]).astype(jnp.bfloat16)
    pre1 = dot(mixed1, w1[...])
    fresh = (pre1 * sigmoid(pre1)).astype(jnp.bfloat16)
    fresh_out[...] = fresh
    copies = spread_rows(1, fresh)
    finish(copies)
    mixed2 = (dot(adj[...], rows[1]) + halo2[...]).astype(jnp.bfloat16)
    pre2 = dot(mixed2, w2[...])
    layer_out[...] = (pre2 * sigmoid(pre2)).astype(jnp.bfloat16)
    back2 = (cot[...].astype(jnp.float32) * silu_slope(pre2)).astype(jnp.bfloat16)
    upstream = dot(back2, w2[...], ((1,), (1,))).astype(jnp.bfloat16)
    copies = spread_rows(2, upstream)
    share[1] = dot(mixed2, back2, ((0,), (0,)))
    finish(copies)
    back1 = (dot(adj[...], rows[2]) * silu_slope(pre1)).astype(jnp.bfloat16)
    share[0] = dot(mixed1, back1, ((0,), (0,)))

    copy = links.copy(share.at[1 - c], from_core, twin)
    copy.wait()
    half[...] = share[c] + from_core[...]
    piece = WIDTH // NX
    copies = []
    for k in range(1, NX):
        start = pl.multiple_of(((x + k) % NX) * piece, piece)
        copies.append(links.copy(half.at[pl.ds(start, piece), :], from_x.at[k - 1], x_peers[k - 1]))
    finish(copies)
    total = half[pl.ds(pl.multiple_of(x * piece, piece), piece), :]
    for k in range(NX - 1):
        total += from_x[k]
    part_x[...] = total
    small = piece // NZ
    copies = []
    for k in range(1, NZ):
        start = pl.multiple_of(((z + k) % NZ) * small, small)
        copies.append(links.copy(part_x.at[pl.ds(start, small), :], from_z.at[k - 1], z_peers[k - 1]))
    finish(copies)
    total = part_x[pl.ds(pl.multiple_of(z * small, small), small), :]
    for k in range(NZ - 1):
        total += from_z[k]
    from_y[y] = total
    finish([links.copy(from_y.at[y], from_y.at[y], peer) for peer in y_peers])
    total = from_y[0]
    for k in range(1, NY):
        total += from_y[k]
    at_z = pl.ds(pl.multiple_of(z * small, small), small)
    whole_z[at_z, :] = total
    finish([links.copy(whole_z.at[at_z, :], whole_z.at[at_z, :], peer) for peer in z_peers])
    at_x = pl.ds(pl.multiple_of(x * piece, piece), piece)
    whole_x[c, at_x, :] = whole_z[...]
    finish([links.copy(whole_x.at[c, at_x, :], whole_x.at[c, at_x, :], peer) for peer in x_peers])
    finish([links.copy(whole_x.at[c], whole_x.at[c], twin)])
    grad1[...] = whole_x[0]
    grad2[...] = whole_x[1]


def run_tail(features, halo1, halo2, inner_adj, weight1, weight2, cot):
    f32, bf16 = jnp.float32, jnp.bfloat16
    piece, small = WIDTH // NX, WIDTH // NX // NZ
    n_copies = 3 * 3 + 1 + 3 + 7 + 7 + 7 + 3 + 1
    vmem = pl.BlockSpec(memory_space=pltpu.VMEM)
    return pl.pallas_call(
        tail_kernel,
        out_shape=(
            jax.ShapeDtypeStruct((ROWS, WIDTH), bf16),
            jax.ShapeDtypeStruct((ROWS, WIDTH), bf16),
            jax.ShapeDtypeStruct((WIDTH, WIDTH), f32),
            jax.ShapeDtypeStruct((WIDTH, WIDTH), f32),
        ),
        in_specs=[vmem] * 7,
        out_specs=(vmem,) * 4,
        scratch_shapes=[
            pltpu.VMEM((3, NX * ROWS, WIDTH), bf16),
            pltpu.VMEM((2, WIDTH, WIDTH), f32),
            pltpu.VMEM((WIDTH, WIDTH), f32),
            pltpu.VMEM((WIDTH, WIDTH), f32),
            pltpu.VMEM((NX - 1, piece, WIDTH), f32),
            pltpu.VMEM((piece, WIDTH), f32),
            pltpu.VMEM((NZ - 1, small, WIDTH), f32),
            pltpu.VMEM((small, WIDTH), f32),
            pltpu.VMEM((NY, small, WIDTH), f32),
            pltpu.VMEM((piece, WIDTH), f32),
            pltpu.VMEM((2, WIDTH, WIDTH), f32),
            pltpu.SemaphoreType.DMA((n_copies,)),
            pltpu.SemaphoreType.DMA((n_copies,)),
        ],
        compiler_params=pltpu.CompilerParams(
            collective_id=0, has_side_effects=True, vmem_limit_bytes=32 * 1024 * 1024
        ),
        name="tail",
    )(features, halo1, halo2, inner_adj, weight1, weight2, cot)


def per_device(
    features,
    history,
    inner_adj,
    halo_tiles,
    tile_target,
    pair_counts,
    send_blocks,
    weight1,
    weight2,
    out_cotangent,
):
    n_dom = lax.axis_size("dom")
    n_row = lax.axis_size("row")
    width = features.shape[1]
    expanded = expand_tiles(halo_tiles, tile_target[0], pair_counts[0], inner_adj.shape[0])

    def halo_sum(source):
        halo = lax.all_to_all(
            lax.all_to_all(
                pick_blocks(source, send_blocks, n_dom, n_row),
                "dom",
                split_axis=0,
                concat_axis=0,
                tiled=True,
            ),
            "row",
            split_axis=1,
            concat_axis=1,
            tiled=True,
        )
        return jnp.dot(expanded, halo.reshape(-1, width), preferred_element_type=jnp.float32)

    return run_tail(
        features, halo_sum(features), halo_sum(history), inner_adj, weight1, weight2, out_cotangent
    )


def solution(mesh):
    spread = P(("dom", "row"), None)
    in_specs = (spread,) * 7 + (P(), P(), spread)
    out_specs = (spread, spread, P(), P())
    return jax.shard_map(
        per_device, mesh=mesh, in_specs=in_specs, out_specs=out_specs, check_vma=False
    )
```

```python
import functools

import jax
import jax.numpy as jnp
from jax import lax
from jax.experimental import pallas as pl
from jax.experimental.pallas import tpu as pltpu
from jax.sharding import PartitionSpec as P

RB = 4
CAP = 2
NY = 8
NZ = 8
NC = 2
NX = 4
ROWS = 128
TILE = 64
CODED = 80
FIRST = 64
FIRST_CUT = 32
LAST_CUT = 96
KEPT = NZ * NX * CAP * RB
WIDTH = 256
MESH = pl.DeviceIdType.MESH


def sigmoid(value):
    return 1.0 / (1.0 + jnp.exp(-value))


def silu_slope(value):
    sig = sigmoid(value)
    return sig * (1.0 + value * (1.0 - sig))


def dot(left, right, dims=((1,), (0,))):
    return lax.dot_general(left, right, (dims, ((), ())), preferred_element_type=jnp.float32)


def position():
    dom = lax.axis_index("dom")
    return dom // (NZ * NC), (dom // NC) % NZ, dom % NC, lax.axis_index("row")


def device(y, z, c, x):
    return ((y * NZ + z) * NC + c, x)


class Links:
    def __init__(self, send, recv):
        self.send, self.recv, self.used = send, recv, 0

    def copy(self, src, dst, target):
        made = pltpu.make_async_remote_copy(
            src_ref=src,
            dst_ref=dst,
            send_sem=self.send.at[self.used],
            recv_sem=self.recv.at[self.used],
            device_id=target,
            device_id_type=MESH,
        )
        self.used += 1
        made.start()
        return made


def iota(shape, dim):
    return lax.broadcasted_iota(jnp.int32, shape, dim)


def one_hot(found):
    return jnp.where(found, 1.0, 0.0).astype(jnp.bfloat16)


def kernel(
    feat, hist, adj, tiles, code, picks, w1, w2, cot,
    fresh_out, layer_out, grad1, grad2,
    held, sb, wanted, chosen, order, codes, edges, twin_edges, seen, blocks,
    for_twin, own_sum, of_twin, parts, got,
    rows, share, half, from_core, from_x, part_x, from_z, from_y, whole_z, whole_x, send, recv,
):
    y, z, c, x = position()
    links = Links(send, recv)
    x_peers = [device(y, z, c, (x + k) % NX) for k in range(1, NX)]
    z_peers = [device(y, (z + k) % NZ, c, x) for k in range(1, NZ)]
    y_peers = [device((y + k) % NY, z, c, x) for k in range(1, NY)]
    twin = device(y, z, 1 - c, x)
    x_up, x_down, z_up, z_down = x_peers[0], x_peers[-1], z_peers[0], z_peers[-1]
    sent = []

    def move(src, dst, target):
        made = links.copy(src, dst, target)
        sent.append(made)
        return made

    def push(ref, target):
        return move(ref, ref, target)

    def arrive(copies):
        for copy in copies:
            copy.wait_recv()

    held[0, z, x] = feat[...]
    held[1, z, x] = hist[...]
    sb[z, x] = picks[...]
    barrier = pltpu.get_barrier_semaphore()
    peers = x_peers + z_peers + y_peers + [twin]
    for peer in peers:
        pl.semaphore_signal(barrier, inc=1, device_id=peer, device_id_type=MESH)
    pl.semaphore_wait(barrier, len(peers))

    top = pl.ds(0, FIRST)
    low = pl.ds(FIRST, ROWS - FIRST)

    def gather(a):
        def both_z(step, ref_up, ref_down):
            return [push(ref_up, z_up), push(ref_down, z_down)]

        def top_z(step):
            up, down = held.at[a, (z + NZ - step + 1) % NZ], held.at[a, (z + step - 1) % NZ]
            if step < NZ // 2:
                return both_z(step, up.at[:, top], down.at[:, top])
            return both_z(step, up.at[pl.ds(0, NX // 2), top], down.at[pl.ds(NX // 2, NX // 2), top])

        def low_z(step):
            up, down = held.at[a, (z + NZ - step + 1) % NZ, x], held.at[a, (z + step - 1) % NZ, x]
            if step < NZ // 2:
                return both_z(step, up.at[low], down.at[low])
            return both_z(
                step, up.at[pl.ds(FIRST, LAST_CUT - FIRST)], down.at[pl.ds(LAST_CUT, ROWS - LAST_CUT)]
            )

        x_left, x_right = (x + NX - 1) % NX, (x + 1) % NX
        tx1 = [push(held.at[a, z, x, top], x_up), push(held.at[a, z, x, top], x_down)]
        lz1 = low_z(1)
        yield
        arrive(tx1)
        tx2 = [
            push(held.at[a, z, x_left, pl.ds(0, FIRST_CUT)], x_up),
            push(held.at[a, z, x_right, pl.ds(FIRST_CUT, FIRST - FIRST_CUT)], x_down),
        ]
        yield
        arrive(lz1)
        lz2 = low_z(2)
        yield
        arrive(tx2)
        tz1 = top_z(1)
        yield
        arrive(lz2)
        lz3 = low_z(3)
        yield
        arrive(lz3)
        lz4 = low_z(4)
        yield
        arrive(tz1)
        tz2 = top_z(2)
        yield
        arrive(lz4)
        lx1 = [push(held.at[a, :, x, low], x_up), push(held.at[a, :, x, low], x_down)]
        yield
        arrive(tz2)
        tz3 = top_z(3)
        yield
        arrive(lx1)
        lx2 = [
            push(held.at[a, :, x_left, pl.ds(FIRST, LAST_CUT - FIRST)], x_up),
            push(held.at[a, :, x_right, pl.ds(LAST_CUT, ROWS - LAST_CUT)], x_down),
        ]
        yield
        arrive(tz3)
        tz4 = top_z(4)
        yield
        arrive(lx2)
        yield
        arrive(tz4)
        yield

    first, second = gather(0), gather(1)

    next(first)
    sb_x = [push(sb.at[z, x], peer) for peer in x_peers]

    span = NZ * NC * NX * CAP * RB
    n = iota((span, span), 1)
    place = ((n >> 5) & 7) * 64 + (((n >> 8) + c) & 1) * 32 + (n & 31)
    order[...] = one_hot(iota((span, span), 0) == place)
    n = iota((ROWS, span), 1)
    block = ((n >> 5) & 7) * 16 + (((n >> 8) + c) & 1) * 8 + ((n & 31) >> 2)
    codes[...] = dot(code[...].astype(jnp.bfloat16), one_hot(iota((ROWS, span), 0) == block))

    def cut(k, carry):
        at = pl.ds(pl.multiple_of(k * span, span), span)
        values = dot(tiles[:, at], order[...]).astype(jnp.bfloat16)
        marks = jnp.broadcast_to(codes[pl.ds(k, 1), :], (CODED - TILE, span)).astype(jnp.bfloat16)
        edges[c, k, 0:TILE, :] = values[:, :KEPT]
        edges[c, k, TILE:CODED, :] = marks[:, :KEPT]
        twin_edges[k, 0:TILE, :] = values[:, KEPT:]
        twin_edges[k, TILE:CODED, :] = marks[:, KEPT:]
        return carry

    next(first)
    lax.fori_loop(0, NY, cut, 0)
    across = move(twin_edges, edges.at[c], twin)
    arrive(sb_x)
    sb_z = [push(sb.at[z], peer) for peer in z_peers]
    next(first)
    next(first)
    arrive([across])
    seen[:, y] = edges[:, y]
    edge_copies = [
        move(edges.at[:, (y + k) % NY], seen.at[:, y], y_peers[k - 1]) for k in range(1, NY)
    ]
    next(first)
    next(first)
    next(second)

    arrive(sb_z)
    r = iota((ROWS, KEPT), 1)
    lane = ((z * NC + ((r >> 4) & 1)) * NX + x) * CAP + ((r >> 2) & 1)
    asked = dot(
        sb[...].reshape(NZ * NX * NY, ROWS).astype(jnp.bfloat16), one_hot(iota((ROWS, KEPT), 0) == lane)
    )
    i, r = iota((KEPT, KEPT), 0), iota((KEPT, KEPT), 1)
    fits = ((i & 7) == (r >> 5)) & (((i >> 3) & 1) == ((r >> 3) & 1))
    wanted[...] = jnp.where(fits, asked, 0.0).astype(jnp.bfloat16)

    def choose(q, carry):
        at = pl.ds(pl.multiple_of(q * 16, 16), 16)
        value = dot(wanted[at, :], jnp.ones((16, KEPT), jnp.bfloat16), ((0,), (0,)))
        r, lane = iota((KEPT, KEPT), 0), iota((KEPT, KEPT), 1)
        goal = lane - ((r >> 3) & 1) * ROWS - (r & 3)
        chosen[q] = one_hot(value * RB == goal.astype(jnp.float32))
        return carry

    lax.fori_loop(0, 16, choose, 0)
    for _ in range(5):
        next(first)
        next(second)
    next(first)
    next(first)
    next(second)

    def full_edges(core, k):
        values = seen[core, k, 0:TILE, :].astype(jnp.float32)
        mark = seen[core, k, TILE:CODED, :].astype(jnp.float32)[0:1, :]
        both = [jnp.where(mark == t, values, 0.0).astype(jnp.bfloat16) for t in range(ROWS // TILE)]
        return jnp.concatenate(both, axis=0)

    def partial_sums(a, between):
        def pick(q, carry):
            source = held[a, q // 2, pl.ds((q % 2) * 2, 2)].reshape(KEPT, WIDTH)
            value = dot(chosen[q], source).astype(jnp.bfloat16)
            blocks[:, pl.ds(pl.multiple_of(q * 16, 16), 16), :] = value.reshape(16, 16, WIDTH)
            return carry

        lax.fori_loop(0, 16, pick, 0)
        between()

        def twins(k, carry):
            value = dot(full_edges(1 - c, k), blocks[k * NC + 1 - c])
            for_twin[a, k] = value.astype(jnp.bfloat16)
            return carry

        lax.fori_loop(0, NY, twins, 0)
        crossing = move(for_twin.at[a], of_twin.at[a], twin)
        between()

        def own(k, carry):
            own_sum[k] = dot(full_edges(c, k), blocks[k * NC + c])
            return carry

        lax.fori_loop(0, NY, own, 0)
        between()
        arrive([crossing])
        copies = []
        for k in (4, 3, 5, 2, 6, 1, 7):
            to = (y + k) % NY
            parts[a, to] = (own_sum[to] + of_twin[a, to].astype(jnp.float32)).astype(jnp.bfloat16)
            copies.append(move(parts.at[a, to], got.at[a, y], y_peers[k - 1]))
        got[a, y] = (own_sum[y] + of_twin[a, y].astype(jnp.float32)).astype(jnp.bfloat16)
        return copies

    def halo_sum(a):
        total = got[a, 0].astype(jnp.float32)
        for k in range(1, NY):
            total += got[a, k].astype(jnp.float32)
        return total

    arrive(edge_copies)
    first_parts = partial_sums(0, lambda: next(second))
    for _ in second:
        pass
    second_parts = partial_sums(1, lambda: None)

    mine = pl.ds(pl.multiple_of(x * ROWS, ROWS), ROWS)

    def spread_rows(slot, value):
        rows[slot, mine, :] = value
        return [push(rows.at[slot, mine, :], peer) for peer in x_peers]

    inner1 = dot(adj[...], held[0, z].reshape(NX * ROWS, WIDTH))
    arrive(first_parts)
    mixed1 = (inner1 + halo_sum(0)).astype(jnp.bfloat16)
    pre1 = dot(mixed1, w1[...])
    fresh = (pre1 * sigmoid(pre1)).astype(jnp.bfloat16)
    fresh_out[...] = fresh
    copies = spread_rows(0, fresh)
    arrive(copies)
    inner2 = dot(adj[...], rows[0])
    arrive(second_parts)
    mixed2 = (inner2 + halo_sum(1)).astype(jnp.bfloat16)
    pre2 = dot(mixed2, w2[...])
    layer_out[...] = (pre2 * sigmoid(pre2)).astype(jnp.bfloat16)
    back2 = (cot[...].astype(jnp.float32) * silu_slope(pre2)).astype(jnp.bfloat16)
    upstream = dot(back2, w2[...], ((1,), (1,))).astype(jnp.bfloat16)
    copies = spread_rows(1, upstream)
    share[1] = dot(mixed2, back2, ((0,), (0,)))
    arrive(copies)
    back1 = (dot(adj[...], rows[1]) * silu_slope(pre1)).astype(jnp.bfloat16)
    share[0] = dot(mixed1, back1, ((0,), (0,)))

    arrive([move(share.at[1 - c], from_core, twin)])
    half[...] = share[c] + from_core[...]
    piece = WIDTH // NX
    copies = []
    for k in range(1, NX):
        start = pl.multiple_of(((x + k) % NX) * piece, piece)
        copies.append(move(half.at[pl.ds(start, piece), :], from_x.at[k - 1], x_peers[k - 1]))
    arrive(copies)
    total = half[pl.ds(pl.multiple_of(x * piece, piece), piece), :]
    for k in range(NX - 1):
        total += from_x[k]
    part_x[...] = total
    small = piece // NZ
    copies = []
    for k in range(1, NZ):
        start = pl.multiple_of(((z + k) % NZ) * small, small)
        copies.append(move(part_x.at[pl.ds(start, small), :], from_z.at[k - 1], z_peers[k - 1]))
    arrive(copies)
    total = part_x[pl.ds(pl.multiple_of(z * small, small), small), :]
    for k in range(NZ - 1):
        total += from_z[k]
    from_y[y] = total
    arrive([push(from_y.at[y], peer) for peer in y_peers])
    total = from_y[0]
    for k in range(1, NY):
        total += from_y[k]
    at_z = pl.ds(pl.multiple_of(z * small, small), small)
    whole_z[at_z, :] = total
    arrive([push(whole_z.at[at_z, :], peer) for peer in z_peers])
    at_x = pl.ds(pl.multiple_of(x * piece, piece), piece)
    whole_x[c, at_x, :] = whole_z[...]
    arrive([push(whole_x.at[c, at_x, :], peer) for peer in x_peers])
    arrive([push(whole_x.at[c], twin)])
    grad1[...] = whole_x[0]
    grad2[...] = whole_x[1]
    for copy in sent:
        copy.wait_send()


def per_device(
    features,
    history,
    inner_adj,
    halo_tiles,
    tile_target,
    pair_counts,
    send_blocks,
    weight1,
    weight2,
    out_cotangent,
):
    f32, bf16 = jnp.float32, jnp.bfloat16
    counts = jnp.repeat(pair_counts[0], CAP)
    usable = jnp.arange(counts.shape[0], dtype=jnp.int32) % CAP < counts
    code = jnp.where(usable, tile_target[0], -1).astype(f32).reshape(NY, ROWS)
    picks = send_blocks.astype(f32).reshape(NY, ROWS)
    piece, small = WIDTH // NX, WIDTH // NX // NZ
    span = NZ * NC * NX * CAP * RB
    n_copies = 200
    vmem = pl.BlockSpec(memory_space=pltpu.VMEM)
    return pl.pallas_call(
        kernel,
        out_shape=(
            jax.ShapeDtypeStruct((ROWS, WIDTH), bf16),
            jax.ShapeDtypeStruct((ROWS, WIDTH), bf16),
            jax.ShapeDtypeStruct((WIDTH, WIDTH), f32),
            jax.ShapeDtypeStruct((WIDTH, WIDTH), f32),
        ),
        in_specs=[vmem] * 9,
        out_specs=(vmem,) * 4,
        scratch_shapes=[
            pltpu.VMEM((2, NZ, NX, ROWS, WIDTH), bf16),
            pltpu.VMEM((NZ, NX, NY, ROWS), f32),
            pltpu.VMEM((KEPT, KEPT), bf16),
            pltpu.VMEM((16, KEPT, KEPT), bf16),
            pltpu.VMEM((span, span), bf16),
            pltpu.VMEM((NY, span), f32),
            pltpu.VMEM((NC, NY, CODED, KEPT), bf16),
            pltpu.VMEM((NY, CODED, KEPT), bf16),
            pltpu.VMEM((NC, NY, CODED, KEPT), bf16),
            pltpu.VMEM((NY * NC, KEPT, WIDTH), bf16),
            pltpu.VMEM((2, NY, ROWS, WIDTH), bf16),
            pltpu.VMEM((NY, ROWS, WIDTH), f32),
            pltpu.VMEM((2, NY, ROWS, WIDTH), bf16),
            pltpu.VMEM((2, NY, ROWS, WIDTH), bf16),
            pltpu.VMEM((2, NY, ROWS, WIDTH), bf16),
            pltpu.VMEM((2, NX * ROWS, WIDTH), bf16),
            pltpu.VMEM((2, WIDTH, WIDTH), f32),
            pltpu.VMEM((WIDTH, WIDTH), f32),
            pltpu.VMEM((WIDTH, WIDTH), f32),
            pltpu.VMEM((NX - 1, piece, WIDTH), f32),
            pltpu.VMEM((piece, WIDTH), f32),
            pltpu.VMEM((NZ - 1, small, WIDTH), f32),
            pltpu.VMEM((NY, small, WIDTH), f32),
            pltpu.VMEM((piece, WIDTH), f32),
            pltpu.VMEM((2, WIDTH, WIDTH), f32),
            pltpu.SemaphoreType.DMA((n_copies,)),
            pltpu.SemaphoreType.DMA((n_copies,)),
        ],
        compiler_params=pltpu.CompilerParams(
            collective_id=0, has_side_effects=True, vmem_limit_bytes=48 * 1024 * 1024
        ),
        name="layers",
    )(features, history, inner_adj, halo_tiles, code, picks, weight1, weight2, out_cotangent)


def solution(mesh):
    spread = P(("dom", "row"), None)
    in_specs = (spread,) * 7 + (P(), P(), spread)
    out_specs = (spread, spread, P(), P())
    return jax.shard_map(
        per_device, mesh=mesh, in_specs=in_specs, out_specs=out_specs, check_vma=False
    )
```

```python
import functools

import jax
import jax.numpy as jnp
from jax import lax
from jax.experimental import pallas as pl
from jax.experimental.pallas import tpu as pltpu
from jax.sharding import PartitionSpec as P

RB = 4
CAP = 2
NY = 8
NZ = 8
NC = 2
NX = 4
ROWS = 128
TILE = 64
CODED = 80
FIRST = 48
FIRST_CUT = 32
LAST_CUT = 96
NEAR_FAR = (4, 3, 5, 2, 6, 1, 7, 0)
KEPT = NZ * NX * CAP * RB
WIDTH = 256
MESH = pl.DeviceIdType.MESH


def sigmoid(value):
    return 1.0 / (1.0 + jnp.exp(-value))


def silu_slope(value):
    sig = sigmoid(value)
    return sig * (1.0 + value * (1.0 - sig))


def dot(left, right, dims=((1,), (0,))):
    return lax.dot_general(left, right, (dims, ((), ())), preferred_element_type=jnp.float32)


def position():
    dom = lax.axis_index("dom")
    return dom // (NZ * NC), (dom // NC) % NZ, dom % NC, lax.axis_index("row")


def device(y, z, c, x):
    return ((y * NZ + z) * NC + c, x)


class Links:
    def __init__(self, send, recv):
        self.send, self.recv, self.used = send, recv, 0

    def copy(self, src, dst, target):
        made = pltpu.make_async_remote_copy(
            src_ref=src,
            dst_ref=dst,
            send_sem=self.send.at[self.used],
            recv_sem=self.recv.at[self.used],
            device_id=target,
            device_id_type=MESH,
        )
        self.used += 1
        made.start()
        return made


def iota(shape, dim):
    return lax.broadcasted_iota(jnp.int32, shape, dim)


def one_hot(found):
    return jnp.where(found, 1.0, 0.0).astype(jnp.bfloat16)


def kernel(
    feat, hist, adj_in, tiles_in, target_in, counts_in, sends_in, w1_in, w2_in, cot_in,
    fresh_out, layer_out, grad1, grad2,
    adj, tiles, target, counts, sends, w1, w2, cot, layer,
    held, sb, code, used, wanted, chosen, order, codes, edges, twin_edges, seen, blocks,
    for_twin, of_twin, parts, got,
    rows, share, rounded, from_group, part, from_z, from_y, whole, final, grads, send, recv, near,
):
    y, z, c, x = position()
    links = Links(send, recv)
    x_peers = [device(y, z, c, (x + k) % NX) for k in range(1, NX)]
    z_peers = [device(y, (z + k) % NZ, c, x) for k in range(1, NZ)]
    y_peers = [device((y + k) % NY, z, c, x) for k in range(1, NY)]
    twin = device(y, z, 1 - c, x)
    across_peers = [device(y, z, 1 - c, (x + k) % NX) for k in range(1, NX)]
    x_up, x_down, z_up, z_down = x_peers[0], x_peers[-1], z_peers[0], z_peers[-1]
    sent = []
    local = []

    def move(src, dst, target):
        made = links.copy(src, dst, target)
        sent.append(made)
        return made

    def push(ref, target):
        return move(ref, ref, target)

    def arrive(copies):
        for copy in copies:
            copy.wait_recv()

    def here(src, dst):
        made = pltpu.make_async_copy(src, dst, near.at[len(local)])
        made.start()
        local.append(made)
        return made

    barrier = pltpu.get_barrier_semaphore()
    peers = x_peers + z_peers + y_peers + [twin] + across_peers
    for peer in peers:
        pl.semaphore_signal(barrier, inc=1, device_id=peer, device_id_type=MESH)
    load_feat = here(feat, held.at[0, z, x])
    load_sends = here(sends_in, sends)
    load_tiles = here(tiles_in, tiles)
    load_target = here(target_in, target)
    load_counts = here(counts_in, counts)
    load_hist = here(hist, held.at[1, z, x])
    later = [here(a, b) for a, b in ((adj_in, adj), (w1_in, w1), (w2_in, w2), (cot_in, cot))]

    top = pl.ds(0, FIRST)
    low = pl.ds(FIRST, ROWS - FIRST)
    low_first = pl.ds(FIRST, LAST_CUT - FIRST)
    low_last = pl.ds(LAST_CUT, ROWS - LAST_CUT)
    x_left, x_right = (x + NX - 1) % NX, (x + 1) % NX

    def gather(a):
        def top_z(step):
            up, down = held.at[a, (z + NZ - step + 1) % NZ], held.at[a, (z + step - 1) % NZ]
            if step < NZ // 2:
                return [push(up.at[:, top], z_up), push(down.at[:, top], z_down)]
            halves = pl.ds(0, NX // 2), pl.ds(NX // 2, NX // 2)
            return [push(up.at[halves[0], top], z_up), push(down.at[halves[1], top], z_down)]

        def low_z(step):
            up, down = held.at[a, (z + NZ - step + 1) % NZ, x], held.at[a, (z + step - 1) % NZ, x]
            if step < NZ // 2:
                return [push(up.at[low], z_up), push(down.at[low], z_down)]
            return [push(up.at[low_first], z_up), push(down.at[low_last], z_down)]

        def low_x(steps):
            made = []
            for k in steps:
                at = held.at[a, (z + k) % NZ, x, low]
                made += [push(at, x_up), push(at, x_down)]
            return made

        def low_x_on(steps):
            made = []
            for k in steps:
                at = held.at[a, (z + k) % NZ]
                made += [push(at.at[x_left, low_first], x_up), push(at.at[x_right, low_last], x_down)]
            return made

        lz1 = low_z(1)
        tx1 = [push(held.at[a, z, x, top], x_up), push(held.at[a, z, x, top], x_down)]
        lx1 = {0: low_x([0])}
        lx2 = []
        yield
        arrive(tx1)
        tx2 = [
            push(held.at[a, z, x_left, pl.ds(0, FIRST_CUT)], x_up),
            push(held.at[a, z, x_right, pl.ds(FIRST_CUT, FIRST - FIRST_CUT)], x_down),
        ]
        yield
        arrive(lz1)
        lz2 = low_z(2)
        lx1[1] = low_x([1, 7])
        yield
        arrive(tx2)
        tz1 = top_z(1)
        arrive(lx1[0])
        lx2 += low_x_on([0])
        yield
        arrive(lz2)
        lz3 = low_z(3)
        lx1[2] = low_x([2, 6])
        yield
        arrive(lx1[1])
        lx2 += low_x_on([1, 7])
        arrive(lz3)
        lz4 = low_z(4)
        lx1[3] = low_x([3, 5])
        yield
        arrive(tz1)
        tz2 = top_z(2)
        arrive(lx1[2])
        lx2 += low_x_on([2, 6])
        yield
        arrive(lz4)
        lx1[4] = low_x([4])
        yield
        arrive(tz2)
        tz3 = top_z(3)
        arrive(lx1[3])
        lx2 += low_x_on([3, 5])
        yield
        arrive(lx1[4])
        lx2 += low_x_on([4])
        yield
        arrive(tz3)
        tz4 = top_z(4)
        yield
        arrive(lx2)
        yield
        arrive(tz4)
        yield

    gathers = gather(0), gather(1)

    def step(which):
        for letter in which:
            next(gathers["FH".index(letter)])

    span = NZ * NC * NX * CAP * RB
    n = iota((span, span), 1)
    place = ((n >> 5) & 7) * 64 + (((n >> 8) + c) & 1) * 32 + (n & 31)
    order[...] = one_hot(iota((span, span), 0) == place)
    load_sends.wait()
    for k in range(NY):
        sb[z, x, k : k + 1, :] = sends[:, k * ROWS : (k + 1) * ROWS].astype(jnp.float32)

    pl.semaphore_wait(barrier, len(peers))
    load_feat.wait()
    step("F")
    sb_x = [push(sb.at[z, x], peer) for peer in x_peers]
    load_hist.wait()

    load_target.wait()
    load_counts.wait()
    for k in range(NY):
        code[k : k + 1, :] = target[:, k * ROWS : (k + 1) * ROWS].astype(jnp.float32)
        used[k : k + 1, :] = counts[:, k * TILE : (k + 1) * TILE].astype(jnp.float32)
    pairs = one_hot(iota((TILE, ROWS), 0) == (iota((TILE, ROWS), 1) >> 1))
    usable = (iota((NY, ROWS), 1) & 1).astype(jnp.float32) < dot(used[...].astype(jnp.bfloat16), pairs)
    marked = jnp.where(usable, code[...], -1.0).astype(jnp.bfloat16)
    n = iota((ROWS, span), 1)
    block = ((n >> 5) & 7) * 16 + (((n >> 8) + c) & 1) * 8 + ((n & 31) >> 2)
    codes[...] = dot(marked, one_hot(iota((ROWS, span), 0) == block))
    load_tiles.wait()

    def cut(k, carry):
        at = pl.ds(pl.multiple_of(k * span, span), span)
        values = dot(tiles[:, at], order[...]).astype(jnp.bfloat16)
        marks = jnp.broadcast_to(codes[pl.ds(k, 1), :], (CODED - TILE, span)).astype(jnp.bfloat16)
        edges[c, k, 0:TILE, :] = values[:, :KEPT]
        edges[c, k, TILE:CODED, :] = marks[:, :KEPT]
        twin_edges[k, 0:TILE, :] = values[:, KEPT:]
        twin_edges[k, TILE:CODED, :] = marks[:, KEPT:]
        return carry

    step("F")
    lax.fori_loop(0, NY // 2, cut, 0)
    step("F")
    lax.fori_loop(NY // 2, NY, cut, 0)
    across = move(twin_edges, edges.at[c], twin)
    step("FH")
    arrive(sb_x)
    sb_z = [push(sb.at[z], peer) for peer in z_peers]
    step("FHF")
    arrive([across])
    seen[:, y] = edges[:, y]
    edge_copies = [
        move(edges.at[:, (y + k) % NY], seen.at[:, y], y_peers[k - 1]) for k in range(1, NY)
    ]
    step("HF")

    arrive(sb_z)
    r = iota((ROWS, KEPT), 1)
    lane = ((z * NC + ((r >> 4) & 1)) * NX + x) * CAP + ((r >> 2) & 1)
    asked = dot(
        sb[...].reshape(NZ * NX * NY, ROWS).astype(jnp.bfloat16), one_hot(iota((ROWS, KEPT), 0) == lane)
    )
    i, r = iota((KEPT, KEPT), 0), iota((KEPT, KEPT), 1)
    fits = ((i & 7) == (r >> 5)) & (((i >> 3) & 1) == ((r >> 3) & 1))
    wanted[...] = jnp.where(fits, asked, 0.0).astype(jnp.bfloat16)

    def choose(q, carry):
        at = pl.ds(pl.multiple_of(q * 16, 16), 16)
        value = dot(wanted[at, :], jnp.ones((16, KEPT), jnp.bfloat16), ((0,), (0,)))
        r, lane = iota((KEPT, KEPT), 0), iota((KEPT, KEPT), 1)
        goal = lane - ((r >> 3) & 1) * ROWS - (r & 3)
        chosen[q] = one_hot(value * RB == goal.astype(jnp.float32))
        return carry

    lax.fori_loop(0, 8, choose, 0)
    step("HFH")
    lax.fori_loop(8, 16, choose, 0)
    step("FHFHFHFHF")

    def full_edges(core, k):
        values = seen[core, k, 0:TILE, :].astype(jnp.float32)
        mark = seen[core, k, TILE:CODED, :].astype(jnp.float32)[0:1, :]
        both = [jnp.where(mark == t, values, 0.0).astype(jnp.bfloat16) for t in range(ROWS // TILE)]
        return jnp.concatenate(both, axis=0)

    def partial_sums(a, between):
        def pick(q, carry):
            source = held[a, q // 2, pl.ds((q % 2) * 2, 2)].reshape(KEPT, WIDTH)
            value = dot(chosen[q], source).astype(jnp.bfloat16)
            blocks[:, pl.ds(pl.multiple_of(q * 16, 16), 16), :] = value.reshape(16, 16, WIDTH)
            return carry

        lax.fori_loop(0, 16, pick, 0)
        between()
        crossing = []
        for k in NEAR_FAR:
            to = (y + k) % NY
            for_twin[a, to] = dot(full_edges(1 - c, to), blocks[to * NC + 1 - c]).astype(jnp.bfloat16)
            crossing.append(move(for_twin.at[a, to], of_twin.at[a, to], twin))
        between()
        copies = []
        for k, copy in zip(NEAR_FAR, crossing):
            to = (y + k) % NY
            value = dot(full_edges(c, to), blocks[to * NC + c])
            arrive([copy])
            value = (value + of_twin[a, to].astype(jnp.float32)).astype(jnp.bfloat16)
            if k:
                parts[a, to] = value
                copies.append(move(parts.at[a, to], got.at[a, y], y_peers[k - 1]))
            else:
                got[a, y] = value
        return copies

    def halo_sum(a):
        total = got[a, 0].astype(jnp.float32)
        for k in range(1, NY):
            total += got[a, k].astype(jnp.float32)
        return total

    arrive(edge_copies)
    first_parts = partial_sums(0, lambda: step("H"))
    for _ in gathers[1]:
        pass
    second_parts = partial_sums(1, lambda: None)

    mine = pl.ds(pl.multiple_of(x * ROWS, ROWS), ROWS)

    def spread_rows(slot, value):
        rows[slot, mine, :] = value
        return [push(rows.at[slot, mine, :], peer) for peer in x_peers]

    for copy in later:
        copy.wait()
    inner1 = dot(adj[...], held[0, z].reshape(NX * ROWS, WIDTH))
    arrive(first_parts)
    mixed1 = (inner1 + halo_sum(0)).astype(jnp.bfloat16)
    pre1 = dot(mixed1, w1[...])
    copies = spread_rows(0, (pre1 * sigmoid(pre1)).astype(jnp.bfloat16))
    results = [here(rows.at[0, mine, :], fresh_out)]
    arrive(copies)
    inner2 = dot(adj[...], rows[0])
    arrive(second_parts)
    mixed2 = (inner2 + halo_sum(1)).astype(jnp.bfloat16)
    pre2 = dot(mixed2, w2[...])
    back2 = (cot[...].astype(jnp.float32) * silu_slope(pre2)).astype(jnp.bfloat16)
    upstream = dot(back2, w2[...], ((1,), (1,))).astype(jnp.bfloat16)
    copies = spread_rows(1, upstream)

    group = [(k, 0) for k in range(1, NX)] + [(k, 1) for k in range(NX)]
    group_peers = x_peers + [twin] + across_peers
    piece = WIDTH // len(group_peers + [0])
    own = pl.ds(pl.multiple_of((c * NX + x) * piece, piece), piece)

    def share_out(which, value):
        share[which] = value
        rounded[which] = value.astype(jnp.bfloat16)
        made = []
        for o, (k, flip) in enumerate(group):
            core = (c + flip) % NC
            at = pl.ds(pl.multiple_of((core * NX + (x + k) % NX) * piece, piece), piece)
            made.append(move(rounded.at[which, at, :], from_group.at[which, o], group_peers[o]))
        return made

    shares = share_out(1, dot(mixed2, back2, ((0,), (0,))))
    layer[...] = (pre2 * sigmoid(pre2)).astype(jnp.bfloat16)
    results.append(here(layer, layer_out))
    arrive(copies)
    back1 = (dot(adj[...], rows[1]) * silu_slope(pre1)).astype(jnp.bfloat16)
    shares += share_out(0, dot(mixed1, back1, ((0,), (0,))))
    arrive(shares)
    for which in range(2):
        total = share[which, own, :]
        for o in range(len(group)):
            total += from_group[which, o].astype(jnp.float32)
        part[which * piece : (which + 1) * piece, :] = total
    small = 2 * piece // NZ
    copies = []
    for k in range(1, NZ):
        start = pl.multiple_of(((z + k) % NZ) * small, small)
        copies.append(move(part.at[pl.ds(start, small), :], from_z.at[k - 1], z_peers[k - 1]))
    arrive(copies)
    at_z = pl.ds(pl.multiple_of(z * small, small), small)
    total = part[at_z, :]
    for k in range(NZ - 1):
        total += from_z[k]
    from_y[y] = total
    arrive([push(from_y.at[y], peer) for peer in y_peers])
    total = from_y[0]
    for k in range(1, NY):
        total += from_y[k]
    whole[at_z, :] = total
    arrive([push(whole.at[at_z, :], peer) for peer in z_peers])
    member = c * NX + x
    final[member] = whole[...].astype(jnp.bfloat16)
    arrive([push(final.at[member], peer) for peer in group_peers])
    for m in range(NC * NX):
        for which in range(2):
            piece_of = final[m, which * piece : (which + 1) * piece, :]
            grads[which, m * piece : (m + 1) * piece, :] = piece_of.astype(jnp.float32)
    results += [here(grads.at[0], grad1), here(grads.at[1], grad2)]
    for copy in sent:
        copy.wait_send()
    for copy in results:
        copy.wait()


def keep_kernel(*refs):
    count = (len(refs) - 2) // 3
    into, out = refs[-2:]
    loads = [pltpu.make_async_copy(refs[k], refs[2 * count + k], into.at[k]) for k in range(count)]
    stores = [pltpu.make_async_copy(refs[2 * count + k], refs[count + k], out.at[k]) for k in range(count)]
    for load in loads:
        load.start()
    for load, store in zip(loads, stores):
        load.wait()
        store.start()
    for store in stores:
        store.wait()


def per_device(*arguments):
    f32, bf16, i32 = jnp.float32, jnp.bfloat16, jnp.int32
    piece = WIDTH // (NX * NC)
    span = NZ * NC * NX * CAP * RB
    n_copies = 210
    anywhere = pl.BlockSpec(memory_space=pl.ANY)
    shapes = (
        jax.ShapeDtypeStruct((ROWS, WIDTH), bf16),
        jax.ShapeDtypeStruct((ROWS, WIDTH), bf16),
        jax.ShapeDtypeStruct((WIDTH, WIDTH), f32),
        jax.ShapeDtypeStruct((WIDTH, WIDTH), f32),
    )
    results = pl.pallas_call(
        kernel,
        out_shape=shapes,
        in_specs=[anywhere] * 10,
        out_specs=(anywhere,) * 4,
        scratch_shapes=[
            pltpu.VMEM((ROWS, NX * ROWS), bf16),
            pltpu.VMEM((TILE, NY * span), bf16),
            pltpu.VMEM((1, NY * ROWS), i32),
            pltpu.VMEM((1, NY * TILE), i32),
            pltpu.VMEM((1, NY * ROWS), i32),
            pltpu.VMEM((WIDTH, WIDTH), bf16),
            pltpu.VMEM((WIDTH, WIDTH), bf16),
            pltpu.VMEM((ROWS, WIDTH), bf16),
            pltpu.VMEM((ROWS, WIDTH), bf16),
            pltpu.VMEM((2, NZ, NX, ROWS, WIDTH), bf16),
            pltpu.VMEM((NZ, NX, NY, ROWS), f32),
            pltpu.VMEM((NY, ROWS), f32),
            pltpu.VMEM((NY, TILE), f32),
            pltpu.VMEM((KEPT, KEPT), bf16),
            pltpu.VMEM((16, KEPT, KEPT), bf16),
            pltpu.VMEM((span, span), bf16),
            pltpu.VMEM((NY, span), f32),
            pltpu.VMEM((NC, NY, CODED, KEPT), bf16),
            pltpu.VMEM((NY, CODED, KEPT), bf16),
            pltpu.VMEM((NC, NY, CODED, KEPT), bf16),
            pltpu.VMEM((NY * NC, KEPT, WIDTH), bf16),
            pltpu.VMEM((2, NY, ROWS, WIDTH), bf16),
            pltpu.VMEM((2, NY, ROWS, WIDTH), bf16),
            pltpu.VMEM((2, NY, ROWS, WIDTH), bf16),
            pltpu.VMEM((2, NY, ROWS, WIDTH), bf16),
            pltpu.VMEM((2, NX * ROWS, WIDTH), bf16),
            pltpu.VMEM((2, WIDTH, WIDTH), f32),
            pltpu.VMEM((2, WIDTH, WIDTH), bf16),
            pltpu.VMEM((2, NX * NC - 1, piece, WIDTH), bf16),
            pltpu.VMEM((2 * piece, WIDTH), f32),
            pltpu.VMEM((NZ - 1, 2 * piece // NZ, WIDTH), f32),
            pltpu.VMEM((NY, 2 * piece // NZ, WIDTH), f32),
            pltpu.VMEM((2 * piece, WIDTH), f32),
            pltpu.VMEM((NX * NC, 2 * piece, WIDTH), bf16),
            pltpu.VMEM((2, WIDTH, WIDTH), f32),
            pltpu.SemaphoreType.DMA((n_copies,)),
            pltpu.SemaphoreType.DMA((n_copies,)),
            pltpu.SemaphoreType.DMA((16,)),
        ],
        compiler_params=pltpu.CompilerParams(
            collective_id=0, has_side_effects=True, vmem_limit_bytes=56 * 1024 * 1024
        ),
        name="layers",
    )(*arguments)
    return pl.pallas_call(
        keep_kernel,
        out_shape=shapes,
        in_specs=[anywhere] * 4,
        out_specs=(anywhere,) * 4,
        scratch_shapes=[pltpu.VMEM(shape.shape, shape.dtype) for shape in shapes]
        + [pltpu.SemaphoreType.DMA((4,)), pltpu.SemaphoreType.DMA((4,))],
        compiler_params=pltpu.CompilerParams(vmem_limit_bytes=60 * 1024 * 1024),
        name="keep",
    )(*results)


def solution(mesh):
    spread = P(("dom", "row"), None)
    in_specs = (spread,) * 7 + (P(), P(), spread)
    out_specs = (spread, spread, P(), P())
    return jax.shard_map(
        per_device, mesh=mesh, in_specs=in_specs, out_specs=out_specs, check_vma=False
    )
```

```python
import functools

import jax
import jax.numpy as jnp
from jax import lax
from jax.experimental import pallas as pl
from jax.experimental.pallas import tpu as pltpu
from jax.sharding import PartitionSpec as P

RB = 4
CAP = 2
NY = 8
NZ = 8
NC = 2
NX = 4
ROWS = 128
TILE = 64
CODED = 80
FIRST = 32
LAST_CUT = 80
HALF = ROWS // 2
ORDER = (4, 3, 5, 1, 7, 2, 6, 0)
KEPT = NZ * NX * CAP * RB
WIDTH = 256
MESH = pl.DeviceIdType.MESH


def sigmoid(value):
    return 1.0 / (1.0 + jnp.exp(-value))


def silu_slope(value):
    sig = sigmoid(value)
    return sig * (1.0 + value * (1.0 - sig))


def dot(left, right, dims=((1,), (0,))):
    return lax.dot_general(left, right, (dims, ((), ())), preferred_element_type=jnp.float32)


def position():
    dom = lax.axis_index("dom")
    return dom // (NZ * NC), (dom // NC) % NZ, dom % NC, lax.axis_index("row")


def device(y, z, c, x):
    return ((y * NZ + z) * NC + c, x)


class Links:
    def __init__(self, send, recv):
        self.send, self.recv, self.used = send, recv, 0

    def copy(self, src, dst, target):
        made = pltpu.make_async_remote_copy(
            src_ref=src,
            dst_ref=dst,
            send_sem=self.send.at[self.used],
            recv_sem=self.recv.at[self.used],
            device_id=target,
            device_id_type=MESH,
        )
        self.used += 1
        made.start()
        return made


def iota(shape, dim):
    return lax.broadcasted_iota(jnp.int32, shape, dim)


def one_hot(found):
    return jnp.where(found, 1.0, 0.0).astype(jnp.bfloat16)


def kernel(
    feat, hist, adj_in, tiles_in, target_in, counts_in, sends_in, w1_in, w2_in, cot_in,
    fresh_out, layer_out, grad1, grad2,
    adj, tiles, target, counts, sends, w1, w2, cot, layer,
    held, sb, code, used, chosen, codes, edges, twin_edges, seen, blocks,
    for_twin, of_twin, parts, second_hop, relay3, relay4, got,
    rows, share, rounded, from_group, part, from_z, from_y, whole, final, grads, send, recv, near,
):
    y, z, c, x = position()
    links = Links(send, recv)
    x_peers = [device(y, z, c, (x + k) % NX) for k in range(1, NX)]
    z_peers = [device(y, (z + k) % NZ, c, x) for k in range(1, NZ)]
    y_peers = [device((y + k) % NY, z, c, x) for k in range(1, NY)]
    twin = device(y, z, 1 - c, x)
    across_peers = [device(y, z, 1 - c, (x + k) % NX) for k in range(1, NX)]
    x_up, x_down, z_up, z_down = x_peers[0], x_peers[-1], z_peers[0], z_peers[-1]
    y_up, y_down, y_up2, y_down2 = y_peers[0], y_peers[-1], y_peers[1], y_peers[-2]
    sent = []
    local = []

    def move(src, dst, target):
        made = links.copy(src, dst, target)
        sent.append(made)
        return made

    def push(ref, target):
        return move(ref, ref, target)

    def arrive(copies):
        for copy in copies:
            copy.wait_recv()

    def here(src, dst):
        made = pltpu.make_async_copy(src, dst, near.at[len(local)])
        made.start()
        local.append(made)
        return made

    barrier = pltpu.get_barrier_semaphore()
    peers = x_peers + z_peers + y_peers + [twin] + across_peers
    for peer in peers:
        pl.semaphore_signal(barrier, inc=1, device_id=peer, device_id_type=MESH)
    load_feat = here(feat, held.at[0, z, x])
    load_sends = here(sends_in, sends)
    load_tiles = here(tiles_in, tiles)
    load_target = here(target_in, target)
    load_counts = here(counts_in, counts)
    load_hist = here(hist, held.at[1, z, x])
    later = [here(a, b) for a, b in ((adj_in, adj), (w1_in, w1), (w2_in, w2), (cot_in, cot))]

    top = pl.ds(0, FIRST)
    low = pl.ds(FIRST, ROWS - FIRST)
    low_first = pl.ds(FIRST, LAST_CUT - FIRST)
    low_last = pl.ds(LAST_CUT, ROWS - LAST_CUT)
    x_left, x_right = (x + NX - 1) % NX, (x + 1) % NX
    z_up2, z_down2 = z_peers[1], z_peers[-2]
    before2, after2 = (z + NZ - 2) % NZ, (z + 2) % NZ

    def gather(a):
        def low_x(steps):
            made = []
            for k in steps:
                at = held.at[a, (z + k) % NZ, x, low]
                made += [push(at, x_up), push(at, x_down)]
            return made

        def low_x_on(steps):
            made = []
            for k in steps:
                at = held.at[a, (z + k) % NZ]
                made += [push(at.at[x_left, low_first], x_up), push(at.at[x_right, low_last], x_down)]
            return made

        at = held.at[a, z, x, low]
        lz_far = [push(at, z_up2), push(at, z_down2)]
        tx = [push(held.at[a, z, x, top], peer) for peer in x_peers]
        lz_near = [push(at, z_up), push(at, z_down)]
        lx = {0: low_x([0])}
        ends = []
        yield
        arrive(tx)
        at = held.at[a, z, :, top]
        tz_far = [push(at, z_up2), push(at, z_down2)]
        tz_near = [push(at, z_up), push(at, z_down)]
        yield
        arrive(lz_far)
        up, down = held.at[a, before2, x], held.at[a, after2, x]
        lz_on = [push(up.at[low_first], z_up2), push(down.at[low_last], z_down2)]
        lz_on += [push(up.at[low], z_up), push(down.at[low], z_down)]
        lx[2] = low_x([2, 6])
        yield
        arrive(lz_near)
        lx[1] = low_x([1, 7])
        arrive(lx[0])
        ends += low_x_on([0])
        yield
        arrive(tz_far)
        up, down = held.at[a, before2], held.at[a, after2]
        tz_on = [
            push(up.at[pl.ds(0, NX // 2), top], z_up2),
            push(down.at[pl.ds(NX // 2, NX // 2), top], z_down2),
            push(up.at[:, top], z_up),
            push(down.at[:, top], z_down),
        ]
        yield
        arrive(lz_on)
        lx[3] = low_x([3, 5, 4])
        yield
        arrive(lx[2])
        ends += low_x_on([2, 6])
        arrive(lx[1])
        ends += low_x_on([1, 7])
        yield
        arrive(lx[3])
        ends += low_x_on([3, 5, 4])
        yield
        arrive(tz_near + tz_on + ends)
        yield

    gathers = gather(0), gather(1)

    def step(which):
        for letter in which:
            next(gathers["FH".index(letter)])

    span = NZ * NC * NX * CAP * RB
    n = iota((1, span), 1)
    place = ((n >> 5) & 7) * 64 + (((n >> 8) + c) & 1) * 32 + (n & 31)
    order = one_hot(iota((span, span), 0) == place)
    block = ((n >> 5) & 7) * 16 + (((n >> 8) + c) & 1) * 8 + ((n & 31) >> 2)
    block_order = one_hot(iota((ROWS, span), 0) == block)
    load_sends.wait()
    for k in range(NY):
        sb[z, x, k : k + 1, :] = sends[:, k * ROWS : (k + 1) * ROWS].astype(jnp.float32)
    load_target.wait()
    load_counts.wait()
    for k in range(NY):
        code[k : k + 1, :] = target[:, k * ROWS : (k + 1) * ROWS].astype(jnp.float32)
        used[k : k + 1, :] = counts[:, k * TILE : (k + 1) * TILE].astype(jnp.float32)
    pairs = one_hot(iota((TILE, ROWS), 0) == (iota((1, ROWS), 1) >> 1))
    usable = (iota((1, ROWS), 1) & 1).astype(jnp.float32) < dot(used[...].astype(jnp.bfloat16), pairs)
    marked = jnp.where(usable, code[...], -1.0).astype(jnp.bfloat16)
    codes[...] = dot(marked, block_order)
    load_tiles.wait()
    stacked = jnp.concatenate([tiles[:, k * span : (k + 1) * span] for k in range(NY)], axis=0)
    placed = dot(stacked, order).astype(jnp.bfloat16)
    for k in range(NY):
        values = placed[k * TILE : (k + 1) * TILE]
        marks = jnp.broadcast_to(codes[k : k + 1, :], (CODED - TILE, span)).astype(jnp.bfloat16)
        edges[c, k, 0:TILE, :] = values[:, :KEPT]
        edges[c, k, TILE:CODED, :] = marks[:, :KEPT]
        twin_edges[k, 0:TILE, :] = values[:, KEPT:]
        twin_edges[k, TILE:CODED, :] = marks[:, KEPT:]
    load_feat.wait()
    load_hist.wait()

    pl.semaphore_wait(barrier, len(peers))
    step("F")
    sb_x = [push(sb.at[z, x], peer) for peer in x_peers]
    across = move(twin_edges, edges.at[c], twin)
    arrive([across])
    seen[:, y] = edges[:, y]
    edge_copies = [
        move(edges.at[:, (y + k) % NY], seen.at[:, y], y_peers[k - 1]) for k in range(1, NY)
    ]
    step("FFF")
    arrive(sb_x)
    sb_z = [push(sb.at[z], peer) for peer in z_peers]
    step("HFHF")

    arrive(sb_z)
    r = iota((1, KEPT), 1)
    lane = ((z * NC + ((r >> 4) & 1)) * NX + x) * CAP + ((r >> 2) & 1)
    asked = dot(
        one_hot(iota((ROWS, KEPT), 0) == lane),
        sb[...].reshape(NZ * NX * NY, ROWS).astype(jnp.bfloat16),
        ((0,), (1,)),
    )
    r, i = iota((KEPT, KEPT), 0), iota((KEPT, KEPT), 1)
    fits = ((i & 7) == (r >> 5)) & (((i >> 3) & 1) == ((r >> 3) & 1))
    wanted = jnp.where(fits, asked, 0.0).astype(jnp.bfloat16)
    pair = one_hot((iota((KEPT, ROWS), 0) >> 4) == iota((KEPT, ROWS), 1))
    r = iota((KEPT, 1), 0)
    base = ((r >> 3) & 1) * ROWS + (r & 3)
    slots = dot(wanted, pair) * RB + base.astype(jnp.float32)
    lanes = iota((1, KEPT), 1).astype(jnp.float32)
    for q in range(16):
        chosen[q] = one_hot(slots[:, q : q + 1] == lanes)
    step("HFHFHF")

    def full_edges(core, k):
        values = seen[core, k, 0:TILE, :].astype(jnp.float32)
        mark = seen[core, k, TILE:CODED, :].astype(jnp.float32)[0:1, :]
        both = [jnp.where(mark == t, values, 0.0).astype(jnp.bfloat16) for t in range(ROWS // TILE)]
        return jnp.concatenate(both, axis=0)

    def partial_sums(a, between):
        def pick(q, carry):
            source = held[a, q // 2, pl.ds((q % 2) * 2, 2)].reshape(KEPT, WIDTH)
            value = dot(chosen[q], source).astype(jnp.bfloat16)
            blocks[:, pl.ds(pl.multiple_of(q * 16, 16), 16), :] = value.reshape(16, 16, WIDTH)
            return carry

        lax.fori_loop(0, 16, pick, 0, unroll=4)
        between()
        crossing = []
        for k in ORDER:
            to = (y + k) % NY
            for_twin[a, to] = dot(full_edges(1 - c, to), blocks[to * NC + 1 - c]).astype(jnp.bfloat16)
            crossing.append(move(for_twin.at[a, to], of_twin.at[a, to], twin))
        between()
        relayed, direct = [], []
        for k, copy in zip(ORDER, crossing):
            to = (y + k) % NY
            value = dot(full_edges(c, to), blocks[to * NC + c])
            arrive([copy])
            value += of_twin[a, to].astype(jnp.float32)
            if k == 0:
                got[a, 0] = value.astype(jnp.bfloat16)
                continue
            if k == 2 or k == 6:
                second_hop[a, k // 4] = value
                continue
            parts[a, k] = value.astype(jnp.bfloat16)
            if k == 4:
                for side, to_y in enumerate((y_up2, y_down2)):
                    at = pl.ds(side * HALF, HALF)
                    relayed.append(move(parts.at[a, k, at], relay4.at[a, side], to_y))
            elif k == 3 or k == 5:
                side = 0 if k == 3 else 1
                relayed.append(move(parts.at[a, k], relay3.at[a, side], (y_up, y_down)[side]))
            else:
                side = 0 if k == 1 else 1
                direct.append(move(parts.at[a, k], got.at[a, 1 + side], (y_up, y_down)[side]))

        def relay():
            arrive(relayed)
            for side, to_y in enumerate((y_up2, y_down2)):
                value = second_hop[a, side] + relay3[a, side].astype(jnp.float32)
                far = relay4[a, side].astype(jnp.float32)
                k = 2 if side == 0 else 6
                for at, add in ((0, side == 0), (HALF, side == 1)):
                    rows_of = value[at : at + HALF]
                    parts[a, k, at : at + HALF, :] = (rows_of + far if add else rows_of).astype(jnp.bfloat16)
                direct.append(move(parts.at[a, k], got.at[a, 3 + side], to_y))
            return direct

        return relay

    def halo_sum(a):
        total = got[a, 0].astype(jnp.float32)
        for k in range(1, 5):
            total += got[a, k].astype(jnp.float32)
        return total

    arrive(edge_copies)
    relay_first = partial_sums(0, lambda: step("H"))
    for _ in gathers[1]:
        pass
    first_parts = relay_first()
    relay_second = partial_sums(1, lambda: None)

    mine = pl.ds(pl.multiple_of(x * ROWS, ROWS), ROWS)

    def spread_rows(slot, value):
        rows[slot, mine, :] = value
        return [push(rows.at[slot, mine, :], peer) for peer in x_peers]

    for copy in later:
        copy.wait()
    inner1 = dot(adj[...], held[0, z].reshape(NX * ROWS, WIDTH))
    arrive(first_parts)
    mixed1 = (inner1 + halo_sum(0)).astype(jnp.bfloat16)
    pre1 = dot(mixed1, w1[...])
    copies = spread_rows(0, (pre1 * sigmoid(pre1)).astype(jnp.bfloat16))
    second_parts = relay_second()
    results = [here(rows.at[0, mine, :], fresh_out)]
    arrive(copies)
    inner2 = dot(adj[...], rows[0])
    arrive(second_parts)
    mixed2 = (inner2 + halo_sum(1)).astype(jnp.bfloat16)
    pre2 = dot(mixed2, w2[...])
    back2 = (cot[...].astype(jnp.float32) * silu_slope(pre2)).astype(jnp.bfloat16)
    upstream = dot(back2, w2[...], ((1,), (1,))).astype(jnp.bfloat16)
    copies = spread_rows(1, upstream)

    group = [(k, 0) for k in range(1, NX)] + [(k, 1) for k in range(NX)]
    group_peers = x_peers + [twin] + across_peers
    piece = WIDTH // len(group_peers + [0])
    own = pl.ds(pl.multiple_of((c * NX + x) * piece, piece), piece)

    def share_out(which, value):
        share[which] = value
        rounded[which] = value.astype(jnp.bfloat16)
        made = []
        for o, (k, flip) in enumerate(group):
            core = (c + flip) % NC
            at = pl.ds(pl.multiple_of((core * NX + (x + k) % NX) * piece, piece), piece)
            made.append(move(rounded.at[which, at, :], from_group.at[which, o], group_peers[o]))
        return made

    shares = share_out(1, dot(mixed2, back2, ((0,), (0,))))
    layer[...] = (pre2 * sigmoid(pre2)).astype(jnp.bfloat16)
    results.append(here(layer, layer_out))
    arrive(copies)
    back1 = (dot(adj[...], rows[1]) * silu_slope(pre1)).astype(jnp.bfloat16)
    shares += share_out(0, dot(mixed1, back1, ((0,), (0,))))
    arrive(shares)
    for which in range(2):
        total = share[which, own, :]
        for o in range(len(group)):
            total += from_group[which, o].astype(jnp.float32)
        part[which * piece : (which + 1) * piece, :] = total
    small = 2 * piece // NZ
    copies = []
    for k in range(1, NZ):
        start = pl.multiple_of(((z + k) % NZ) * small, small)
        copies.append(move(part.at[pl.ds(start, small), :], from_z.at[k - 1], z_peers[k - 1]))
    arrive(copies)
    at_z = pl.ds(pl.multiple_of(z * small, small), small)
    total = part[at_z, :]
    for k in range(NZ - 1):
        total += from_z[k]
    from_y[y] = total
    arrive([push(from_y.at[y], peer) for peer in y_peers])
    total = from_y[0]
    for k in range(1, NY):
        total += from_y[k]
    whole[at_z, :] = total
    arrive([push(whole.at[at_z, :], peer) for peer in z_peers])
    member = c * NX + x
    final[member] = whole[...].astype(jnp.bfloat16)
    arrive([push(final.at[member], peer) for peer in group_peers])
    for m in range(NC * NX):
        for which in range(2):
            piece_of = final[m, which * piece : (which + 1) * piece, :]
            grads[which, m * piece : (m + 1) * piece, :] = piece_of.astype(jnp.float32)
    results += [here(grads.at[0], grad1), here(grads.at[1], grad2)]
    for copy in sent:
        copy.wait_send()
    for copy in results:
        copy.wait()


def keep_kernel(*refs):
    count = (len(refs) - 2) // 3
    into, out = refs[-2:]
    loads = [pltpu.make_async_copy(refs[k], refs[2 * count + k], into.at[k]) for k in range(count)]
    stores = [pltpu.make_async_copy(refs[2 * count + k], refs[count + k], out.at[k]) for k in range(count)]
    for load in loads:
        load.start()
    for load, store in zip(loads, stores):
        load.wait()
        store.start()
    for store in stores:
        store.wait()


def per_device(*arguments):
    f32, bf16, i32 = jnp.float32, jnp.bfloat16, jnp.int32
    piece = WIDTH // (NX * NC)
    span = NZ * NC * NX * CAP * RB
    n_copies = 210
    anywhere = pl.BlockSpec(memory_space=pl.ANY)
    shapes = (
        jax.ShapeDtypeStruct((ROWS, WIDTH), bf16),
        jax.ShapeDtypeStruct((ROWS, WIDTH), bf16),
        jax.ShapeDtypeStruct((WIDTH, WIDTH), f32),
        jax.ShapeDtypeStruct((WIDTH, WIDTH), f32),
    )
    results = pl.pallas_call(
        kernel,
        out_shape=shapes,
        in_specs=[anywhere] * 10,
        out_specs=(anywhere,) * 4,
        scratch_shapes=[
            pltpu.VMEM((ROWS, NX * ROWS), bf16),
            pltpu.VMEM((TILE, NY * span), bf16),
            pltpu.VMEM((1, NY * ROWS), i32),
            pltpu.VMEM((1, NY * TILE), i32),
            pltpu.VMEM((1, NY * ROWS), i32),
            pltpu.VMEM((WIDTH, WIDTH), bf16),
            pltpu.VMEM((WIDTH, WIDTH), bf16),
            pltpu.VMEM((ROWS, WIDTH), bf16),
            pltpu.VMEM((ROWS, WIDTH), bf16),
            pltpu.VMEM((2, NZ, NX, ROWS, WIDTH), bf16),
            pltpu.VMEM((NZ, NX, NY, ROWS), f32),
            pltpu.VMEM((NY, ROWS), f32),
            pltpu.VMEM((NY, TILE), f32),
            pltpu.VMEM((16, KEPT, KEPT), bf16),
            pltpu.VMEM((NY, span), f32),
            pltpu.VMEM((NC, NY, CODED, KEPT), bf16),
            pltpu.VMEM((NY, CODED, KEPT), bf16),
            pltpu.VMEM((NC, NY, CODED, KEPT), bf16),
            pltpu.VMEM((NY * NC, KEPT, WIDTH), bf16),
            pltpu.VMEM((2, NY, ROWS, WIDTH), bf16),
            pltpu.VMEM((2, NY, ROWS, WIDTH), bf16),
            pltpu.VMEM((2, NY, ROWS, WIDTH), bf16),
            pltpu.VMEM((2, 2, ROWS, WIDTH), f32),
            pltpu.VMEM((2, 2, ROWS, WIDTH), bf16),
            pltpu.VMEM((2, 2, HALF, WIDTH), bf16),
            pltpu.VMEM((2, 5, ROWS, WIDTH), bf16),
            pltpu.VMEM((2, NX * ROWS, WIDTH), bf16),
            pltpu.VMEM((2, WIDTH, WIDTH), f32),
            pltpu.VMEM((2, WIDTH, WIDTH), bf16),
            pltpu.VMEM((2, NX * NC - 1, piece, WIDTH), bf16),
            pltpu.VMEM((2 * piece, WIDTH), f32),
            pltpu.VMEM((NZ - 1, 2 * piece // NZ, WIDTH), f32),
            pltpu.VMEM((NY, 2 * piece // NZ, WIDTH), f32),
            pltpu.VMEM((2 * piece, WIDTH), f32),
            pltpu.VMEM((NX * NC, 2 * piece, WIDTH), bf16),
            pltpu.VMEM((2, WIDTH, WIDTH), f32),
            pltpu.SemaphoreType.DMA((n_copies,)),
            pltpu.SemaphoreType.DMA((n_copies,)),
            pltpu.SemaphoreType.DMA((16,)),
        ],
        compiler_params=pltpu.CompilerParams(
            collective_id=0, has_side_effects=True, vmem_limit_bytes=56 * 1024 * 1024
        ),
        name="layers",
    )(*arguments)
    return pl.pallas_call(
        keep_kernel,
        out_shape=shapes,
        in_specs=[anywhere] * 4,
        out_specs=(anywhere,) * 4,
        scratch_shapes=[pltpu.VMEM(shape.shape, shape.dtype) for shape in shapes]
        + [pltpu.SemaphoreType.DMA((4,)), pltpu.SemaphoreType.DMA((4,))],
        compiler_params=pltpu.CompilerParams(vmem_limit_bytes=60 * 1024 * 1024),
        name="keep",
    )(*results)


def solution(mesh):
    spread = P(("dom", "row"), None)
    in_specs = (spread,) * 7 + (P(), P(), spread)
    out_specs = (spread, spread, P(), P())
    return jax.shard_map(
        per_device, mesh=mesh, in_specs=in_specs, out_specs=out_specs, check_vma=False
    )
```

```python
import functools

import jax
import jax.numpy as jnp
from jax import lax
from jax.experimental import pallas as pl
from jax.experimental.pallas import tpu as pltpu
from jax.sharding import PartitionSpec as P

RB = 4
CAP = 2
NY = 8
NZ = 8
NC = 2
NX = 4
ROWS = 128
TILE = 64
CODED = 80
FIRST = 32
LAST_CUT = 80
HALF = ROWS // 2
ORDER = (4, 3, 5, 1, 7, 2, 6, 0)
FAR_FIRST = (4, 3, 5, 2, 6, 1, 7)
KEPT = NZ * NX * CAP * RB
WIDTH = 256
MESH = pl.DeviceIdType.MESH


def sigmoid(value):
    return 1.0 / (1.0 + jnp.exp(-value))


def silu_slope(value):
    sig = sigmoid(value)
    return sig * (1.0 + value * (1.0 - sig))


def dot(left, right, dims=((1,), (0,))):
    return lax.dot_general(left, right, (dims, ((), ())), preferred_element_type=jnp.float32)


def position():
    dom = lax.axis_index("dom")
    return dom // (NZ * NC), (dom // NC) % NZ, dom % NC, lax.axis_index("row")


def device(y, z, c, x):
    return ((y * NZ + z) * NC + c, x)


class Links:
    def __init__(self, send, recv):
        self.send, self.recv, self.used = send, recv, 0

    def copy(self, src, dst, target):
        made = pltpu.make_async_remote_copy(
            src_ref=src,
            dst_ref=dst,
            send_sem=self.send.at[self.used],
            recv_sem=self.recv.at[self.used],
            device_id=target,
            device_id_type=MESH,
        )
        self.used += 1
        made.start()
        return made


def iota(shape, dim):
    return lax.broadcasted_iota(jnp.int32, shape, dim)


def one_hot(found):
    return jnp.where(found, 1.0, 0.0).astype(jnp.bfloat16)


def kernel(
    feat, hist, adj_in, tiles_in, target_in, counts_in, sends_in, w1_in, w2_in, cot_in,
    fresh_out, layer_out, grad1, grad2,
    adj, tiles, target, counts, sends, w1, w2, cot, layer,
    held, sb, code, used, chosen, codes, edges, twin_edges, seen, blocks,
    for_twin, of_twin, parts, second_hop, relay3, relay4, got,
    rows, slopes, turned, share, rounded, from_twin, halves, sending, from_row, leaving, arriving, part, from_z, from_y, whole, final, grads, send, recv, near,
):
    y, z, c, x = position()
    links = Links(send, recv)
    x_peers = [device(y, z, c, (x + k) % NX) for k in range(1, NX)]
    z_peers = [device(y, (z + k) % NZ, c, x) for k in range(1, NZ)]
    y_peers = [device((y + k) % NY, z, c, x) for k in range(1, NY)]
    twin = device(y, z, 1 - c, x)
    z_far_first = [z_peers[k - 1] for k in FAR_FIRST]
    y_far_first = [y_peers[k - 1] for k in FAR_FIRST]
    x_up, x_down, z_up, z_down = x_peers[0], x_peers[-1], z_peers[0], z_peers[-1]
    y_up, y_down, y_up2, y_down2 = y_peers[0], y_peers[-1], y_peers[1], y_peers[-2]
    sent = []
    local = []

    def move(src, dst, target):
        made = links.copy(src, dst, target)
        sent.append(made)
        return made

    def push(ref, target):
        return move(ref, ref, target)

    def arrive(copies):
        for copy in copies:
            copy.wait_recv()

    def here(src, dst):
        made = pltpu.make_async_copy(src, dst, near.at[len(local)])
        made.start()
        local.append(made)
        return made

    barrier = pltpu.get_barrier_semaphore()
    peers = [peer for pair in zip(y_far_first, z_far_first) for peer in pair]
    peers += x_peers + [twin]
    for peer in peers:
        pl.semaphore_signal(barrier, inc=1, device_id=peer, device_id_type=MESH)
    load_feat = here(feat, held.at[0, z, x])
    load_sends = here(sends_in, sends)
    load_tiles = here(tiles_in, tiles)
    load_target = here(target_in, target)
    load_counts = here(counts_in, counts)
    load_hist = here(hist, held.at[1, z, x])
    mine = pl.ds(pl.multiple_of(x * ROWS, ROWS), ROWS)
    adj_here = adj.at[mine, :]
    later = [here(a, b) for a, b in ((adj_in, adj_here), (w1_in, w1), (w2_in, w2), (cot_in, cot))]

    top = pl.ds(0, FIRST)
    low = pl.ds(FIRST, ROWS - FIRST)
    low_first = pl.ds(FIRST, LAST_CUT - FIRST)
    low_last = pl.ds(LAST_CUT, ROWS - LAST_CUT)
    x_left, x_right = (x + NX - 1) % NX, (x + 1) % NX
    z_up2, z_down2 = z_peers[1], z_peers[-2]
    before2, after2 = (z + NZ - 2) % NZ, (z + 2) % NZ

    def gather(a):
        def low_x(steps):
            made = []
            for k in steps:
                at = held.at[a, (z + k) % NZ, x, low]
                made += [push(at, x_up), push(at, x_down)]
            return made

        def low_x_on(steps):
            made = []
            for k in steps:
                at = held.at[a, (z + k) % NZ]
                made += [push(at.at[x_left, low_first], x_up), push(at.at[x_right, low_last], x_down)]
            return made

        at = held.at[a, z, x, low]
        lz_far = [push(at, z_up2), push(at, z_down2)]
        tx = [push(held.at[a, z, x, top], peer) for peer in x_peers]
        lz_near = [push(at, z_up), push(at, z_down)]
        lx = {0: low_x([0])}
        ends = []
        yield
        arrive(tx)
        at = held.at[a, z, :, top]
        tz_far = [push(at, z_up2), push(at, z_down2)]
        tz_near = [push(at, z_up), push(at, z_down)]
        yield
        arrive(lz_far)
        up, down = held.at[a, before2, x], held.at[a, after2, x]
        lz_on = [push(up.at[low_first], z_up2), push(down.at[low_last], z_down2)]
        lz_on += [push(up.at[low], z_up), push(down.at[low], z_down)]
        lx[2] = low_x([2, 6])
        yield
        arrive(lz_near)
        lx[1] = low_x([1, 7])
        arrive(lx[0])
        ends += low_x_on([0])
        yield
        arrive(tz_far)
        up, down = held.at[a, before2], held.at[a, after2]
        tz_on = [
            push(up.at[pl.ds(0, NX // 2), top], z_up2),
            push(down.at[pl.ds(NX // 2, NX // 2), top], z_down2),
            push(up.at[:, top], z_up),
            push(down.at[:, top], z_down),
        ]
        yield
        arrive(lz_on)
        lx[3] = low_x([3, 5, 4])
        yield
        arrive(lx[2])
        ends += low_x_on([2, 6])
        arrive(lx[1])
        ends += low_x_on([1, 7])
        yield
        arrive(lx[3])
        ends += low_x_on([3, 5, 4])
        yield
        arrive(tz_near + tz_on + ends)
        yield

    gathers = gather(0), gather(1)

    def step(which):
        for letter in which:
            next(gathers["FH".index(letter)])

    span = NZ * NC * NX * CAP * RB
    n = iota((1, span), 1)
    place = ((n >> 5) & 7) * 64 + (((n >> 8) + c) & 1) * 32 + (n & 31)
    order = one_hot(iota((span, span), 0) == place)
    block = ((n >> 5) & 7) * 16 + (((n >> 8) + c) & 1) * 8 + ((n & 31) >> 2)
    block_order = one_hot(iota((ROWS, span), 0) == block)
    load_sends.wait()
    for k in range(NY):
        sb[z, x, k : k + 1, :] = sends[:, k * ROWS : (k + 1) * ROWS].astype(jnp.float32)
    load_target.wait()
    load_counts.wait()
    for k in range(NY):
        code[k : k + 1, :] = target[:, k * ROWS : (k + 1) * ROWS].astype(jnp.float32)
        used[k : k + 1, :] = counts[:, k * TILE : (k + 1) * TILE].astype(jnp.float32)
    pairs = one_hot(iota((TILE, ROWS), 0) == (iota((1, ROWS), 1) >> 1))
    usable = (iota((1, ROWS), 1) & 1).astype(jnp.float32) < dot(used[...].astype(jnp.bfloat16), pairs)
    marked = jnp.where(usable, code[...], -1.0).astype(jnp.bfloat16)
    codes[...] = dot(marked, block_order)
    load_tiles.wait()
    stacked = jnp.concatenate([tiles[:, k * span : (k + 1) * span] for k in range(NY)], axis=0)
    placed = dot(stacked, order).astype(jnp.bfloat16)
    for k in range(NY):
        values = placed[k * TILE : (k + 1) * TILE]
        marks = jnp.broadcast_to(codes[k : k + 1, :], (CODED - TILE, span)).astype(jnp.bfloat16)
        edges[c, k, 0:TILE, :] = values[:, :KEPT]
        edges[c, k, TILE:CODED, :] = marks[:, :KEPT]
        twin_edges[k, 0:TILE, :] = values[:, KEPT:]
        twin_edges[k, TILE:CODED, :] = marks[:, KEPT:]
    load_feat.wait()
    load_hist.wait()

    pl.semaphore_wait(barrier, len(peers))
    step("F")
    sb_x = [push(sb.at[z, x], peer) for peer in x_peers]
    across = move(twin_edges, edges.at[c], twin)
    arrive([across])
    seen[:, y] = edges[:, y]
    edge_copies = [
        move(edges.at[:, (y + k) % NY], seen.at[:, y], y_peers[k - 1]) for k in FAR_FIRST
    ]
    step("FFF")
    arrive(sb_x)
    sb_z = [push(sb.at[z], peer) for peer in z_far_first]
    step("HFHF")

    arrive(sb_z)
    r = iota((1, KEPT), 1)
    lane = ((z * NC + ((r >> 4) & 1)) * NX + x) * CAP + ((r >> 2) & 1)
    asked = dot(
        one_hot(iota((ROWS, KEPT), 0) == lane),
        sb[...].reshape(NZ * NX * NY, ROWS).astype(jnp.bfloat16),
        ((0,), (1,)),
    )
    r, i = iota((KEPT, KEPT), 0), iota((KEPT, KEPT), 1)
    fits = ((i & 7) == (r >> 5)) & (((i >> 3) & 1) == ((r >> 3) & 1))
    wanted = jnp.where(fits, asked, 0.0).astype(jnp.bfloat16)
    pair = one_hot((iota((KEPT, ROWS), 0) >> 4) == iota((KEPT, ROWS), 1))
    r = iota((KEPT, 1), 0)
    base = ((r >> 3) & 1) * ROWS + (r & 3)
    slots = dot(wanted, pair) * RB + base.astype(jnp.float32)
    lanes = iota((1, KEPT), 1).astype(jnp.float32)
    for q in range(16):
        chosen[q] = one_hot(slots[:, q : q + 1] == lanes)
    step("HFHFHF")

    def full_edges(core, k):
        values = seen[core, k, 0:TILE, :].astype(jnp.float32)
        mark = seen[core, k, TILE:CODED, :].astype(jnp.float32)[0:1, :]
        both = [jnp.where(mark == t, values, 0.0).astype(jnp.bfloat16) for t in range(ROWS // TILE)]
        return jnp.concatenate(both, axis=0)

    def partial_sums(a, between):
        def pick(q, carry):
            source = held[a, q // 2, pl.ds((q % 2) * 2, 2)].reshape(KEPT, WIDTH)
            value = dot(chosen[q], source).astype(jnp.bfloat16)
            blocks[:, pl.ds(pl.multiple_of(q * 16, 16), 16), :] = value.reshape(16, 16, WIDTH)
            return carry

        lax.fori_loop(0, 16, pick, 0, unroll=4)
        between()
        crossing = []
        for k in ORDER:
            to = (y + k) % NY
            for_twin[a, to] = dot(full_edges(1 - c, to), blocks[to * NC + 1 - c]).astype(jnp.bfloat16)
            crossing.append(move(for_twin.at[a, to], of_twin.at[a, to], twin))
        between()
        relayed, direct = [], []
        for k, copy in zip(ORDER, crossing):
            to = (y + k) % NY
            value = dot(full_edges(c, to), blocks[to * NC + c])
            arrive([copy])
            value += of_twin[a, to].astype(jnp.float32)
            if k == 0:
                got[a, 0] = value.astype(jnp.bfloat16)
                continue
            if k == 2 or k == 6:
                second_hop[a, k // 4] = value
                continue
            parts[a, k] = value.astype(jnp.bfloat16)
            if k == 4:
                for side, to_y in enumerate((y_up2, y_down2)):
                    at = pl.ds(side * HALF, HALF)
                    relayed.append(move(parts.at[a, k, at], relay4.at[a, side], to_y))
            elif k == 3 or k == 5:
                side = 0 if k == 3 else 1
                relayed.append(move(parts.at[a, k], relay3.at[a, side], (y_up, y_down)[side]))
            else:
                side = 0 if k == 1 else 1
                direct.append(move(parts.at[a, k], got.at[a, 1 + side], (y_up, y_down)[side]))

        def relay():
            arrive(relayed)
            for side, to_y in enumerate((y_up2, y_down2)):
                value = second_hop[a, side] + relay3[a, side].astype(jnp.float32)
                far = relay4[a, side].astype(jnp.float32)
                k = 2 if side == 0 else 6
                for at, add in ((0, side == 0), (HALF, side == 1)):
                    rows_of = value[at : at + HALF]
                    parts[a, k, at : at + HALF, :] = (rows_of + far if add else rows_of).astype(jnp.bfloat16)
                direct.append(move(parts.at[a, k], got.at[a, 3 + side], to_y))
            return direct

        return relay

    def halo_sum(a):
        total = got[a, 0].astype(jnp.float32)
        for k in range(1, 5):
            total += got[a, k].astype(jnp.float32)
        return total

    arrive(edge_copies)
    relay_first = partial_sums(0, lambda: step("H"))
    for _ in gathers[1]:
        pass
    for copy in later:
        copy.wait()
    adj_copies = [push(adj_here, peer) for peer in x_peers]
    first_parts = relay_first()
    relay_second = partial_sums(1, lambda: None)

    def spread_rows(slot, value):
        rows[slot, mine, :] = value
        return [push(rows.at[slot, mine, :], peer) for peer in x_peers]

    inner1 = dot(adj[mine, :], held[0, z].reshape(NX * ROWS, WIDTH))
    arrive(first_parts)
    mixed1 = (inner1 + halo_sum(0)).astype(jnp.bfloat16)
    pre1 = dot(mixed1, w1[...])
    copies = spread_rows(0, (pre1 * sigmoid(pre1)).astype(jnp.bfloat16))
    second_parts = relay_second()
    results = [here(rows.at[0, mine, :], fresh_out)]
    slopes[x] = silu_slope(pre1).astype(jnp.bfloat16)
    turned[x] = mixed1.T
    arrive(copies)
    row_copies = [push(ref.at[x], peer) for ref in (turned, slopes) for peer in x_peers]
    inner2 = dot(adj[mine, :], rows[0])
    arrive(second_parts)
    mixed2 = (inner2 + halo_sum(1)).astype(jnp.bfloat16)
    pre2 = dot(mixed2, w2[...])
    back2 = (cot[...].astype(jnp.float32) * silu_slope(pre2)).astype(jnp.bfloat16)
    upstream = dot(back2, w2[...], ((1,), (1,))).astype(jnp.bfloat16)
    copies = spread_rows(1, upstream)

    half = WIDTH // NC
    piece = half // NX
    kept = pl.ds(pl.multiple_of(c * half, half), half)
    given = pl.ds(pl.multiple_of((1 - c) * half, half), half)

    def to_row(crossing):
        arrive([crossing])
        value = share[kept, :] + from_twin[...].astype(jnp.float32)
        halves[...] = value
        sending[...] = value.astype(jnp.bfloat16)
        made = []
        for k in (2, 1, 3):
            at = pl.ds(pl.multiple_of((x + k) % NX * piece, piece), piece)
            made.append(move(sending.at[at, :], from_row.at[k - 1], x_peers[k - 1]))
        return made

    share[...] = dot(mixed2, back2, ((0,), (0,)))
    rounded[...] = share[...].astype(jnp.bfloat16)
    crossing = move(rounded.at[given, :], from_twin, twin)
    layer[...] = (pre2 * sigmoid(pre2)).astype(jnp.bfloat16)
    results.append(here(layer, layer_out))
    shares = to_row(crossing)
    arrive(shares)
    own = pl.ds(pl.multiple_of(x * piece, piece), piece)
    total = halves[own, :]
    for k in range(NX - 1):
        total += from_row[k].astype(jnp.float32)
    part[piece : 2 * piece, :] = total

    arrive(adj_copies)
    arrive(row_copies)
    arrive(copies)
    spread = dot(adj[...], rows[1])
    slope = slopes[...].reshape(NX * ROWS, WIDTH).astype(jnp.float32)
    back1 = (spread * slope).astype(jnp.bfloat16)

    def turned_rows(core):
        at = pl.ds(pl.multiple_of(core * half + x * piece, piece), piece)
        return jnp.concatenate([turned[k, at, :] for k in range(NX)], axis=1)

    first_grad = dot(jnp.concatenate([turned_rows(1 - c), turned_rows(c)], axis=0), back1)
    leaving[...] = first_grad[:piece].astype(jnp.bfloat16)
    arrive([move(leaving, arriving, twin)])
    part[0:piece, :] = first_grad[piece:] + arriving[...].astype(jnp.float32)
    small = 2 * piece // NZ
    copies = []
    for k in FAR_FIRST:
        start = pl.multiple_of(((z + k) % NZ) * small, small)
        copies.append(move(part.at[pl.ds(start, small), :], from_z.at[k - 1], z_peers[k - 1]))
    arrive(copies)
    at_z = pl.ds(pl.multiple_of(z * small, small), small)
    total = part[at_z, :]
    for k in range(NZ - 1):
        total += from_z[k]
    from_y[y] = total
    arrive([push(from_y.at[y], peer) for peer in y_far_first])
    total = from_y[0]
    for k in range(1, NY):
        total += from_y[k]
    whole[at_z, :] = total
    arrive([push(whole.at[at_z, :], peer) for peer in z_far_first])
    final[c, x] = whole[...].astype(jnp.bfloat16)
    copies = [push(final.at[c, x], x_peers[k - 1]) for k in (2, 1, 3)]
    crossings = [push(final.at[c, x], twin)]
    for k, copy in zip((2, 1, 3), copies):
        arrive([copy])
        crossings.append(push(final.at[c, (x + NX - k) % NX], twin))

    def unpack(core):
        for m in range(NX):
            for which in range(2):
                at = pl.ds(pl.multiple_of(core * half + m * piece, piece), piece)
                value = final[core, m, which * piece : (which + 1) * piece, :]
                grads[which, at, :] = value.astype(jnp.float32)

    unpack(c)
    arrive(crossings)
    unpack(1 - c)
    results += [here(grads.at[0], grad1), here(grads.at[1], grad2)]
    for copy in sent:
        copy.wait_send()
    for copy in results:
        copy.wait()


def keep_kernel(*refs):
    count = (len(refs) - 2) // 3
    into, out = refs[-2:]
    loads = [pltpu.make_async_copy(refs[k], refs[2 * count + k], into.at[k]) for k in range(count)]
    stores = [pltpu.make_async_copy(refs[2 * count + k], refs[count + k], out.at[k]) for k in range(count)]
    for load in loads:
        load.start()
    for load, store in zip(loads, stores):
        load.wait()
        store.start()
    for store in stores:
        store.wait()


def per_device(*arguments):
    f32, bf16, i32 = jnp.float32, jnp.bfloat16, jnp.int32
    piece = WIDTH // (NX * NC)
    span = NZ * NC * NX * CAP * RB
    n_copies = 210
    anywhere = pl.BlockSpec(memory_space=pl.ANY)
    shapes = (
        jax.ShapeDtypeStruct((ROWS, WIDTH), bf16),
        jax.ShapeDtypeStruct((ROWS, WIDTH), bf16),
        jax.ShapeDtypeStruct((WIDTH, WIDTH), f32),
        jax.ShapeDtypeStruct((WIDTH, WIDTH), f32),
    )
    results = pl.pallas_call(
        kernel,
        out_shape=shapes,
        in_specs=[anywhere] * 10,
        out_specs=(anywhere,) * 4,
        scratch_shapes=[
            pltpu.VMEM((NX * ROWS, NX * ROWS), bf16),
            pltpu.VMEM((TILE, NY * span), bf16),
            pltpu.VMEM((1, NY * ROWS), i32),
            pltpu.VMEM((1, NY * TILE), i32),
            pltpu.VMEM((1, NY * ROWS), i32),
            pltpu.VMEM((WIDTH, WIDTH), bf16),
            pltpu.VMEM((WIDTH, WIDTH), bf16),
            pltpu.VMEM((ROWS, WIDTH), bf16),
            pltpu.VMEM((ROWS, WIDTH), bf16),
            pltpu.VMEM((2, NZ, NX, ROWS, WIDTH), bf16),
            pltpu.VMEM((NZ, NX, NY, ROWS), f32),
            pltpu.VMEM((NY, ROWS), f32),
            pltpu.VMEM((NY, TILE), f32),
            pltpu.VMEM((16, KEPT, KEPT), bf16),
            pltpu.VMEM((NY, span), f32),
            pltpu.VMEM((NC, NY, CODED, KEPT), bf16),
            pltpu.VMEM((NY, CODED, KEPT), bf16),
            pltpu.VMEM((NC, NY, CODED, KEPT), bf16),
            pltpu.VMEM((NY * NC, KEPT, WIDTH), bf16),
            pltpu.VMEM((2, NY, ROWS, WIDTH), bf16),
            pltpu.VMEM((2, NY, ROWS, WIDTH), bf16),
            pltpu.VMEM((2, NY, ROWS, WIDTH), bf16),
            pltpu.VMEM((2, 2, ROWS, WIDTH), f32),
            pltpu.VMEM((2, 2, ROWS, WIDTH), bf16),
            pltpu.VMEM((2, 2, HALF, WIDTH), bf16),
            pltpu.VMEM((2, 5, ROWS, WIDTH), bf16),
            pltpu.VMEM((2, NX * ROWS, WIDTH), bf16),
            pltpu.VMEM((NX, ROWS, WIDTH), bf16),
            pltpu.VMEM((NX, WIDTH, ROWS), bf16),
            pltpu.VMEM((WIDTH, WIDTH), f32),
            pltpu.VMEM((WIDTH, WIDTH), bf16),
            pltpu.VMEM((WIDTH // NC, WIDTH), bf16),
            pltpu.VMEM((WIDTH // NC, WIDTH), f32),
            pltpu.VMEM((WIDTH // NC, WIDTH), bf16),
            pltpu.VMEM((NX - 1, piece, WIDTH), bf16),
            pltpu.VMEM((piece, WIDTH), bf16),
            pltpu.VMEM((piece, WIDTH), bf16),
            pltpu.VMEM((2 * piece, WIDTH), f32),
            pltpu.VMEM((NZ - 1, 2 * piece // NZ, WIDTH), f32),
            pltpu.VMEM((NY, 2 * piece // NZ, WIDTH), f32),
            pltpu.VMEM((2 * piece, WIDTH), f32),
            pltpu.VMEM((NC, NX, 2 * piece, WIDTH), bf16),
            pltpu.VMEM((2, WIDTH, WIDTH), f32),
            pltpu.SemaphoreType.DMA((n_copies,)),
            pltpu.SemaphoreType.DMA((n_copies,)),
            pltpu.SemaphoreType.DMA((16,)),
        ],
        compiler_params=pltpu.CompilerParams(
            collective_id=0, has_side_effects=True, vmem_limit_bytes=56 * 1024 * 1024
        ),
        name="layers",
    )(*arguments)
    return pl.pallas_call(
        keep_kernel,
        out_shape=shapes,
        in_specs=[anywhere] * 4,
        out_specs=(anywhere,) * 4,
        scratch_shapes=[pltpu.VMEM(shape.shape, shape.dtype) for shape in shapes]
        + [pltpu.SemaphoreType.DMA((4,)), pltpu.SemaphoreType.DMA((4,))],
        compiler_params=pltpu.CompilerParams(vmem_limit_bytes=60 * 1024 * 1024),
        name="keep",
    )(*results)


def solution(mesh):
    spread = P(("dom", "row"), None)
    in_specs = (spread,) * 7 + (P(), P(), spread)
    out_specs = (spread, spread, P(), P())
    return jax.shard_map(
        per_device, mesh=mesh, in_specs=in_specs, out_specs=out_specs, check_vma=False
    )
```

```python
import functools

import jax
import jax.numpy as jnp
from jax import lax
from jax.experimental import pallas as pl
from jax.experimental.pallas import tpu as pltpu
from jax.sharding import PartitionSpec as P

RB = 4
CAP = 2
NY = 8
NZ = 8
NC = 2
NX = 4
ROWS = 128
TILE = 64
CODED = 80
FIRST = 32
LAST_CUT = 80
HALF = ROWS // 2
ORDER = (4, 3, 5, 1, 7, 2, 6, 0)
FAR_FIRST = (4, 3, 5, 2, 6, 1, 7)
KEPT = NZ * NX * CAP * RB
WIDTH = 256
MESH = pl.DeviceIdType.MESH


def sigmoid(value):
    return 1.0 / (1.0 + jnp.exp(-value))


def silu_slope(value):
    sig = sigmoid(value)
    return sig * (1.0 + value * (1.0 - sig))


def dot(left, right, dims=((1,), (0,))):
    return lax.dot_general(left, right, (dims, ((), ())), preferred_element_type=jnp.float32)


def position():
    dom = lax.axis_index("dom")
    return dom // (NZ * NC), (dom // NC) % NZ, dom % NC, lax.axis_index("row")


def device(y, z, c, x):
    return ((y * NZ + z) * NC + c, x)


class Links:
    def __init__(self, send, recv):
        self.send, self.recv, self.used = send, recv, 0

    def copy(self, src, dst, target):
        made = pltpu.make_async_remote_copy(
            src_ref=src,
            dst_ref=dst,
            send_sem=self.send.at[self.used],
            recv_sem=self.recv.at[self.used],
            device_id=target,
            device_id_type=MESH,
        )
        self.used += 1
        made.start()
        return made


def iota(shape, dim):
    return lax.broadcasted_iota(jnp.int32, shape, dim)


def one_hot(found):
    return jnp.where(found, 1.0, 0.0).astype(jnp.bfloat16)


def kernel(
    feat, hist, adj_in, tiles_in, target_in, counts_in, sends_in, w1_in, w2_in, cot_in,
    fresh_out, layer_out, grad1, grad2,
    adj, tiles, target, counts, sends, w1, w2, w2_t, cot, layer,
    held, sb, code, used, chosen, codes, edges, twin_edges, seen, blocks,
    for_twin, of_twin, parts, second_hop, relay3, relay4, got,
    rows, slopes, turned, share, rounded, from_twin, halves, sending, from_row, leaving, arriving, part, folded, from_z, from_y, final, grads, send, recv, near,
):
    y, z, c, x = position()
    links = Links(send, recv)
    x_peers = [device(y, z, c, (x + k) % NX) for k in range(1, NX)]
    z_peers = [device(y, (z + k) % NZ, c, x) for k in range(1, NZ)]
    y_peers = [device((y + k) % NY, z, c, x) for k in range(1, NY)]
    twin = device(y, z, 1 - c, x)
    z_far_first = [z_peers[k - 1] for k in FAR_FIRST]
    y_far_first = [y_peers[k - 1] for k in FAR_FIRST]
    x_up, x_down, z_up, z_down = x_peers[0], x_peers[-1], z_peers[0], z_peers[-1]
    y_up, y_down, y_up2, y_down2 = y_peers[0], y_peers[-1], y_peers[1], y_peers[-2]
    sent = []
    local = []

    def move(src, dst, target):
        made = links.copy(src, dst, target)
        sent.append(made)
        return made

    def push(ref, target):
        return move(ref, ref, target)

    def arrive(copies):
        for copy in copies:
            copy.wait_recv()

    def settle(leave):
        while len(sent) > leave:
            sent.pop(0).wait_send()

    def here(src, dst):
        made = pltpu.make_async_copy(src, dst, near.at[len(local)])
        made.start()
        local.append(made)
        return made

    barrier = pltpu.get_barrier_semaphore()
    peers = [peer for pair in zip(y_far_first, z_far_first) for peer in pair]
    peers += x_peers + [twin]
    for peer in peers:
        pl.semaphore_signal(barrier, inc=1, device_id=peer, device_id_type=MESH)
    load_feat = here(feat, held.at[0, z, x])
    load_sends = here(sends_in, sends)
    load_tiles = here(tiles_in, tiles)
    load_target = here(target_in, target)
    load_counts = here(counts_in, counts)
    load_hist = here(hist, held.at[1, z, x])
    mine = pl.ds(pl.multiple_of(x * ROWS, ROWS), ROWS)
    adj_here = adj.at[mine, :]
    later = [here(a, b) for a, b in ((adj_in, adj_here), (w1_in, w1), (w2_in, w2), (cot_in, cot))]

    top = pl.ds(0, FIRST)
    low = pl.ds(FIRST, ROWS - FIRST)
    low_first = pl.ds(FIRST, LAST_CUT - FIRST)
    low_last = pl.ds(LAST_CUT, ROWS - LAST_CUT)
    x_left, x_right = (x + NX - 1) % NX, (x + 1) % NX
    z_up2, z_down2 = z_peers[1], z_peers[-2]
    before2, after2 = (z + NZ - 2) % NZ, (z + 2) % NZ

    def gather(a):
        def low_x(steps):
            made = []
            for k in steps:
                at = held.at[a, (z + k) % NZ, x, low]
                made += [push(at, x_up), push(at, x_down)]
            return made

        def low_x_on(steps):
            made = []
            for k in steps:
                at = held.at[a, (z + k) % NZ]
                made += [push(at.at[x_left, low_first], x_up), push(at.at[x_right, low_last], x_down)]
            return made

        at = held.at[a, z, x, low]
        lz_far = [push(at, z_up2), push(at, z_down2)]
        tx = [push(held.at[a, z, x, top], peer) for peer in x_peers]
        lz_near = [push(at, z_up), push(at, z_down)]
        lx = {0: low_x([0])}
        ends = []
        yield
        arrive(tx)
        at = held.at[a, z, :, top]
        tz_far = [push(at, z_up2), push(at, z_down2)]
        tz_near = [push(at, z_up), push(at, z_down)]
        yield
        arrive(lz_far)
        up, down = held.at[a, before2, x], held.at[a, after2, x]
        lz_on = [push(up.at[low_first], z_up2), push(down.at[low_last], z_down2)]
        lz_on += [push(up.at[low], z_up), push(down.at[low], z_down)]
        lx[2] = low_x([2, 6])
        yield
        arrive(lz_near)
        lx[1] = low_x([1, 7])
        arrive(lx[0])
        ends += low_x_on([0])
        yield
        arrive(tz_far)
        up, down = held.at[a, before2], held.at[a, after2]
        tz_on = [
            push(up.at[pl.ds(0, NX // 2), top], z_up2),
            push(down.at[pl.ds(NX // 2, NX // 2), top], z_down2),
            push(up.at[:, top], z_up),
            push(down.at[:, top], z_down),
        ]
        yield
        arrive(lz_on)
        lx[3] = low_x([3, 5, 4])
        yield
        arrive(lx[2])
        ends += low_x_on([2, 6])
        arrive(lx[1])
        ends += low_x_on([1, 7])
        yield
        arrive(lx[3])
        ends += low_x_on([3, 5, 4])
        yield
        arrive(tz_near + tz_on + ends)
        yield

    gathers = gather(0), gather(1)

    def step(which):
        for letter in which:
            next(gathers["FH".index(letter)])

    span = NZ * NC * NX * CAP * RB
    n = iota((1, span), 1)
    place = ((n >> 5) & 7) * 64 + (((n >> 8) + c) & 1) * 32 + (n & 31)
    order = one_hot(iota((span, span), 0) == place)
    block = ((n >> 5) & 7) * 16 + (((n >> 8) + c) & 1) * 8 + ((n & 31) >> 2)
    block_order = one_hot(iota((ROWS, span), 0) == block)
    load_sends.wait()
    for k in range(NY):
        sb[z, x, k : k + 1, :] = sends[:, k * ROWS : (k + 1) * ROWS].astype(jnp.float32)
    load_target.wait()
    load_counts.wait()
    for k in range(NY):
        code[k : k + 1, :] = target[:, k * ROWS : (k + 1) * ROWS].astype(jnp.float32)
        used[k : k + 1, :] = counts[:, k * TILE : (k + 1) * TILE].astype(jnp.float32)
    pairs = one_hot(iota((TILE, ROWS), 0) == (iota((1, ROWS), 1) >> 1))
    usable = (iota((1, ROWS), 1) & 1).astype(jnp.float32) < dot(used[...].astype(jnp.bfloat16), pairs)
    marked = jnp.where(usable, code[...], -1.0).astype(jnp.bfloat16)
    codes[...] = dot(marked, block_order)
    load_tiles.wait()
    stacked = jnp.concatenate([tiles[:, k * span : (k + 1) * span] for k in range(NY)], axis=0)
    placed = dot(stacked, order).astype(jnp.bfloat16)
    for k in range(NY):
        values = placed[k * TILE : (k + 1) * TILE]
        marks = jnp.broadcast_to(codes[k : k + 1, :], (CODED - TILE, span)).astype(jnp.bfloat16)
        edges[c, k, 0:TILE, :] = values[:, :KEPT]
        edges[c, k, TILE:CODED, :] = marks[:, :KEPT]
        twin_edges[k, 0:TILE, :] = values[:, KEPT:]
        twin_edges[k, TILE:CODED, :] = marks[:, KEPT:]
    load_feat.wait()
    load_hist.wait()

    pl.semaphore_wait(barrier, len(peers))
    step("F")
    sb_x = [push(sb.at[z, x], peer) for peer in x_peers]
    across = move(twin_edges, edges.at[c], twin)
    arrive([across])
    seen[:, y] = edges[:, y]
    edge_copies = [
        move(edges.at[:, (y + k) % NY], seen.at[:, y], y_peers[k - 1]) for k in FAR_FIRST
    ]
    step("FFF")
    arrive(sb_x)
    sb_z = [push(sb.at[z], peer) for peer in z_far_first]
    step("HFHF")

    arrive(sb_z)
    r = iota((1, KEPT), 1)
    lane = ((z * NC + ((r >> 4) & 1)) * NX + x) * CAP + ((r >> 2) & 1)
    asked = dot(
        one_hot(iota((ROWS, KEPT), 0) == lane),
        sb[...].reshape(NZ * NX * NY, ROWS).astype(jnp.bfloat16),
        ((0,), (1,)),
    )
    r, i = iota((KEPT, KEPT), 0), iota((KEPT, KEPT), 1)
    fits = ((i & 7) == (r >> 5)) & (((i >> 3) & 1) == ((r >> 3) & 1))
    wanted = jnp.where(fits, asked, 0.0).astype(jnp.bfloat16)
    pair = one_hot((iota((KEPT, ROWS), 0) >> 4) == iota((KEPT, ROWS), 1))
    r = iota((KEPT, 1), 0)
    base = ((r >> 3) & 1) * ROWS + (r & 3)
    slots = dot(wanted, pair) * RB + base.astype(jnp.float32)
    lanes = iota((1, KEPT), 1).astype(jnp.float32)
    for q in range(16):
        chosen[q] = one_hot(slots[:, q : q + 1] == lanes)
    step("HFHFHF")

    def full_edges(core, k):
        values = seen[core, k, 0:TILE, :].astype(jnp.float32)
        mark = seen[core, k, TILE:CODED, :].astype(jnp.float32)[0:1, :]
        both = [jnp.where(mark == t, values, 0.0).astype(jnp.bfloat16) for t in range(ROWS // TILE)]
        return jnp.concatenate(both, axis=0)

    def partial_sums(a, between):
        def pick(q, carry):
            source = held[a, q // 2, pl.ds((q % 2) * 2, 2)].reshape(KEPT, WIDTH)
            value = dot(chosen[q], source).astype(jnp.bfloat16)
            blocks[:, pl.ds(pl.multiple_of(q * 16, 16), 16), :] = value.reshape(16, 16, WIDTH)
            return carry

        lax.fori_loop(0, 16, pick, 0, unroll=4)
        between()
        crossing = []
        for k in ORDER:
            to = (y + k) % NY
            for_twin[a, to] = dot(full_edges(1 - c, to), blocks[to * NC + 1 - c]).astype(jnp.bfloat16)
            crossing.append(move(for_twin.at[a, to], of_twin.at[a, to], twin))
        between()
        relayed, direct = [], []
        for k, copy in zip(ORDER, crossing):
            to = (y + k) % NY
            value = dot(full_edges(c, to), blocks[to * NC + c])
            arrive([copy])
            value += of_twin[a, to].astype(jnp.float32)
            if k == 0:
                got[a, 0] = value.astype(jnp.bfloat16)
                continue
            if k == 2 or k == 6:
                second_hop[a, k // 4] = value
                continue
            parts[a, k] = value.astype(jnp.bfloat16)
            if k == 4:
                for side, to_y in enumerate((y_up2, y_down2)):
                    at = pl.ds(side * HALF, HALF)
                    relayed.append(move(parts.at[a, k, at], relay4.at[a, side], to_y))
            elif k == 3 or k == 5:
                side = 0 if k == 3 else 1
                relayed.append(move(parts.at[a, k], relay3.at[a, side], (y_up, y_down)[side]))
            else:
                side = 0 if k == 1 else 1
                direct.append(move(parts.at[a, k], got.at[a, 1 + side], (y_up, y_down)[side]))

        def relay():
            arrive(relayed)
            for side, to_y in enumerate((y_up2, y_down2)):
                value = second_hop[a, side] + relay3[a, side].astype(jnp.float32)
                far = relay4[a, side].astype(jnp.float32)
                k = 2 if side == 0 else 6
                for at, add in ((0, side == 0), (HALF, side == 1)):
                    rows_of = value[at : at + HALF]
                    parts[a, k, at : at + HALF, :] = (rows_of + far if add else rows_of).astype(jnp.bfloat16)
                direct.append(move(parts.at[a, k], got.at[a, 3 + side], to_y))
            return direct

        return relay

    def near_sum(a, total, copies):
        arrive(copies[:2])
        for k in range(3):
            total += got[a, k].astype(jnp.float32)
        return total

    def halo_sum(a, total, copies):
        arrive(copies[2:])
        return total + (got[a, 3].astype(jnp.float32) + got[a, 4].astype(jnp.float32))

    arrive(edge_copies)

    relay_first = partial_sums(0, lambda: step("H"))
    for _ in gathers[1]:
        pass
    for copy in later:
        copy.wait()
    adj_copies = [push(adj_here, peer) for peer in x_peers]
    first_parts = relay_first()
    relay_second = partial_sums(1, lambda: None)

    def spread_rows(slot, value):
        rows[slot, mine, :] = value
        return [push(rows.at[slot, mine, :], peer) for peer in x_peers]

    inner1 = dot(adj[mine, :], held[0, z].reshape(NX * ROWS, WIDTH))
    sum1 = near_sum(0, inner1, first_parts)
    mixed1 = halo_sum(0, sum1, first_parts).astype(jnp.bfloat16)
    pre1 = dot(mixed1, w1[...])
    copies = spread_rows(0, (pre1 * sigmoid(pre1)).astype(jnp.bfloat16))
    second_parts = relay_second()
    results = [here(rows.at[0, mine, :], fresh_out)]
    slopes[x] = silu_slope(pre1).astype(jnp.bfloat16)
    turned[x] = mixed1.T
    settle(40)
    arrive(copies)
    row_copies = [push(ref.at[x], peer) for ref in (turned, slopes) for peer in x_peers]
    inner2 = dot(adj[mine, :], rows[0])
    w2_t[...] = w2[...].T
    sum2 = near_sum(1, inner2, second_parts)
    mixed2 = halo_sum(1, sum2, second_parts).astype(jnp.bfloat16)
    pre2 = dot(mixed2, w2[...])
    back2 = (cot[...].astype(jnp.float32) * silu_slope(pre2)).astype(jnp.bfloat16)
    upstream = dot(back2, w2_t[...]).astype(jnp.bfloat16)
    copies = spread_rows(1, upstream)

    half = WIDTH // NC
    piece = half // NX
    kept = pl.ds(pl.multiple_of(c * half, half), half)
    given = pl.ds(pl.multiple_of((1 - c) * half, half), half)

    def to_row(crossing):
        arrive([crossing])
        value = share[kept, :] + from_twin[...].astype(jnp.float32)
        halves[...] = value
        sending[...] = value.astype(jnp.bfloat16)
        made = []
        for k in (2, 1, 3):
            at = pl.ds(pl.multiple_of((x + k) % NX * piece, piece), piece)
            made.append(move(sending.at[at, :], from_row.at[k - 1], x_peers[k - 1]))
        return made

    share[...] = dot(mixed2, back2, ((0,), (0,)))
    rounded[...] = share[...].astype(jnp.bfloat16)
    crossing = move(rounded.at[given, :], from_twin, twin)
    layer[...] = (pre2 * sigmoid(pre2)).astype(jnp.bfloat16)
    results.append(here(layer, layer_out))
    shares = to_row(crossing)
    settle(8)
    arrive(shares)
    own = pl.ds(pl.multiple_of(x * piece, piece), piece)
    total = halves[own, :]
    for k in range(NX - 1):
        total += from_row[k].astype(jnp.float32)
    part[piece : 2 * piece, :] = total

    arrive(adj_copies)
    arrive(row_copies)
    arrive(copies)
    spread = dot(adj[...], rows[1])
    slope = slopes[...].reshape(NX * ROWS, WIDTH).astype(jnp.float32)
    back1 = (spread * slope).astype(jnp.bfloat16)

    def turned_rows(core):
        at = pl.ds(pl.multiple_of(core * half + x * piece, piece), piece)
        return jnp.concatenate([turned[k, at, :] for k in range(NX)], axis=1)

    first_grad = dot(jnp.concatenate([turned_rows(1 - c), turned_rows(c)], axis=0), back1)
    leaving[...] = first_grad[:piece].astype(jnp.bfloat16)
    arrive([move(leaving, arriving, twin)])
    part[0:piece, :] = first_grad[piece:] + arriving[...].astype(jnp.float32)
    small = 2 * piece // NZ
    lanes = WIDTH // 2

    def fold(value):
        return jnp.concatenate([value[:, :lanes], value[:, lanes:]], axis=0).astype(jnp.bfloat16)

    for k in range(NZ):
        folded[k] = fold(part[k * small : (k + 1) * small, :])
    copies = []
    for k in FAR_FIRST:
        copies.append(move(folded.at[(z + k) % NZ], from_z.at[k - 1], z_peers[k - 1]))
    settle(7)
    arrive(copies)
    total = folded[z].astype(jnp.float32)
    for k in range(NZ - 1):
        total += from_z[k].astype(jnp.float32)
    from_y[y] = total.astype(jnp.bfloat16)
    copies = [push(from_y.at[y], peer) for peer in y_far_first]
    settle(7)
    arrive(copies)
    total = from_y[0].astype(jnp.float32)
    for k in range(1, NY):
        total += from_y[k].astype(jnp.float32)
    final[c, x, z] = total.astype(jnp.bfloat16)
    copies = [push(final.at[c, x, z], peer) for peer in z_far_first]
    settle(7)
    arrive(copies)
    copies = [push(final.at[c, x], x_peers[k - 1]) for k in (2, 1, 3)]
    crossings = [push(final.at[c, x], twin)]
    settle(4)
    for k, copy in zip((2, 1, 3), copies):
        arrive([copy])
        crossings.append(push(final.at[c, (x + NX - k) % NX], twin))

    def unpack(core):
        for m in range(NX):
            for k in range(NZ):
                which, row = divmod(k * small, piece)
                at = pl.ds(pl.multiple_of(core * half + m * piece + row, small), small)
                value = final[core, m, k].astype(jnp.float32)
                grads[which, at, 0:lanes] = value[:small]
                grads[which, at, lanes:WIDTH] = value[small:]

    unpack(c)
    arrive(crossings)
    unpack(1 - c)
    results += [here(grads.at[0], grad1), here(grads.at[1], grad2)]
    settle(0)
    for copy in results:
        copy.wait()


def keep_kernel(*refs):
    count = (len(refs) - 2) // 3
    into, out = refs[-2:]
    loads = [pltpu.make_async_copy(refs[k], refs[2 * count + k], into.at[k]) for k in range(count)]
    stores = [pltpu.make_async_copy(refs[2 * count + k], refs[count + k], out.at[k]) for k in range(count)]
    for load in loads:
        load.start()
    for load, store in zip(loads, stores):
        load.wait()
        store.start()
    for store in stores:
        store.wait()


def per_device(*arguments):
    f32, bf16, i32 = jnp.float32, jnp.bfloat16, jnp.int32
    piece = WIDTH // (NX * NC)
    span = NZ * NC * NX * CAP * RB
    n_copies = 210
    anywhere = pl.BlockSpec(memory_space=pl.ANY)
    shapes = (
        jax.ShapeDtypeStruct((ROWS, WIDTH), bf16),
        jax.ShapeDtypeStruct((ROWS, WIDTH), bf16),
        jax.ShapeDtypeStruct((WIDTH, WIDTH), f32),
        jax.ShapeDtypeStruct((WIDTH, WIDTH), f32),
    )
    results = pl.pallas_call(
        kernel,
        out_shape=shapes,
        in_specs=[anywhere] * 10,
        out_specs=(anywhere,) * 4,
        scratch_shapes=[
            pltpu.VMEM((NX * ROWS, NX * ROWS), bf16),
            pltpu.VMEM((TILE, NY * span), bf16),
            pltpu.VMEM((1, NY * ROWS), i32),
            pltpu.VMEM((1, NY * TILE), i32),
            pltpu.VMEM((1, NY * ROWS), i32),
            pltpu.VMEM((WIDTH, WIDTH), bf16),
            pltpu.VMEM((WIDTH, WIDTH), bf16),
            pltpu.VMEM((WIDTH, WIDTH), bf16),
            pltpu.VMEM((ROWS, WIDTH), bf16),
            pltpu.VMEM((ROWS, WIDTH), bf16),
            pltpu.VMEM((2, NZ, NX, ROWS, WIDTH), bf16),
            pltpu.VMEM((NZ, NX, NY, ROWS), f32),
            pltpu.VMEM((NY, ROWS), f32),
            pltpu.VMEM((NY, TILE), f32),
            pltpu.VMEM((16, KEPT, KEPT), bf16),
            pltpu.VMEM((NY, span), f32),
            pltpu.VMEM((NC, NY, CODED, KEPT), bf16),
            pltpu.VMEM((NY, CODED, KEPT), bf16),
            pltpu.VMEM((NC, NY, CODED, KEPT), bf16),
            pltpu.VMEM((NY * NC, KEPT, WIDTH), bf16),
            pltpu.VMEM((2, NY, ROWS, WIDTH), bf16),
            pltpu.VMEM((2, NY, ROWS, WIDTH), bf16),
            pltpu.VMEM((2, NY, ROWS, WIDTH), bf16),
            pltpu.VMEM((2, 2, ROWS, WIDTH), f32),
            pltpu.VMEM((2, 2, ROWS, WIDTH), bf16),
            pltpu.VMEM((2, 2, HALF, WIDTH), bf16),
            pltpu.VMEM((2, 5, ROWS, WIDTH), bf16),
            pltpu.VMEM((2, NX * ROWS, WIDTH), bf16),
            pltpu.VMEM((NX, ROWS, WIDTH), bf16),
            pltpu.VMEM((NX, WIDTH, ROWS), bf16),
            pltpu.VMEM((WIDTH, WIDTH), f32),
            pltpu.VMEM((WIDTH, WIDTH), bf16),
            pltpu.VMEM((WIDTH // NC, WIDTH), bf16),
            pltpu.VMEM((WIDTH // NC, WIDTH), f32),
            pltpu.VMEM((WIDTH // NC, WIDTH), bf16),
            pltpu.VMEM((NX - 1, piece, WIDTH), bf16),
            pltpu.VMEM((piece, WIDTH), bf16),
            pltpu.VMEM((piece, WIDTH), bf16),
            pltpu.VMEM((2 * piece, WIDTH), f32),
            pltpu.VMEM((NZ, 4 * piece // NZ, WIDTH // 2), bf16),
            pltpu.VMEM((NZ - 1, 4 * piece // NZ, WIDTH // 2), bf16),
            pltpu.VMEM((NY, 4 * piece // NZ, WIDTH // 2), bf16),
            pltpu.VMEM((NC, NX, NZ, 4 * piece // NZ, WIDTH // 2), bf16),
            pltpu.VMEM((2, WIDTH, WIDTH), f32),
            pltpu.SemaphoreType.DMA((n_copies,)),
            pltpu.SemaphoreType.DMA((n_copies,)),
            pltpu.SemaphoreType.DMA((16,)),
        ],
        compiler_params=pltpu.CompilerParams(
            collective_id=0, has_side_effects=True, vmem_limit_bytes=56 * 1024 * 1024
        ),
        name="layers",
    )(*arguments)
    return pl.pallas_call(
        keep_kernel,
        out_shape=shapes,
        in_specs=[anywhere] * 4,
        out_specs=(anywhere,) * 4,
        scratch_shapes=[pltpu.VMEM(shape.shape, shape.dtype) for shape in shapes]
        + [pltpu.SemaphoreType.DMA((4,)), pltpu.SemaphoreType.DMA((4,))],
        compiler_params=pltpu.CompilerParams(vmem_limit_bytes=60 * 1024 * 1024),
        name="keep",
    )(*results)


def solution(mesh):
    spread = P(("dom", "row"), None)
    in_specs = (spread,) * 7 + (P(), P(), spread)
    out_specs = (spread, spread, P(), P())
    return jax.shard_map(
        per_device, mesh=mesh, in_specs=in_specs, out_specs=out_specs, check_vma=False
    )
```

```python
import functools

import jax
import jax.numpy as jnp
from jax import lax
from jax.experimental import pallas as pl
from jax.experimental.pallas import tpu as pltpu
from jax.sharding import PartitionSpec as P

RB = 4
CAP = 2
NY = 8
NZ = 8
NC = 2
NX = 4
ROWS = 128
TILE = 64
CODED = 80
FIRST = 32
LAST_CUT = 80
HALF = ROWS // 2
ORDER = (4, 3, 5, 1, 7, 2, 6, 0)
FAR_FIRST = (4, 3, 5, 2, 6, 1, 7)
KEPT = NZ * NX * CAP * RB
WIDTH = 256
MESH = pl.DeviceIdType.MESH


def sigmoid(value):
    return 1.0 / (1.0 + jnp.exp(-value))


def silu_slope(value):
    sig = sigmoid(value)
    return sig * (1.0 + value * (1.0 - sig))


def dot(left, right, dims=((1,), (0,))):
    return lax.dot_general(left, right, (dims, ((), ())), preferred_element_type=jnp.float32)


def position():
    dom = lax.axis_index("dom")
    return dom // (NZ * NC), (dom // NC) % NZ, dom % NC, lax.axis_index("row")


def device(y, z, c, x):
    return ((y * NZ + z) * NC + c, x)


class Links:
    def __init__(self, send, recv):
        self.send, self.recv, self.used = send, recv, 0

    def copy(self, src, dst, target):
        made = pltpu.make_async_remote_copy(
            src_ref=src,
            dst_ref=dst,
            send_sem=self.send.at[self.used],
            recv_sem=self.recv.at[self.used],
            device_id=target,
            device_id_type=MESH,
        )
        self.used += 1
        made.start()
        return made


def iota(shape, dim):
    return lax.broadcasted_iota(jnp.int32, shape, dim)


def one_hot(found):
    return jnp.where(found, 1.0, 0.0).astype(jnp.bfloat16)


def kernel(
    feat, hist, adj_in, tiles_in, target_in, counts_in, sends_in, w1_in, w2_in, cot_in,
    fresh_out, layer_out, final_out,
    adj, tiles, target, counts, sends, w1, w2, w2_t, cot, layer,
    held, sb, code, used, chosen, codes, edges, twin_edges, seen, blocks,
    for_twin, of_twin, parts, second_hop, relay3, relay4, got,
    rows, slopes, turned, share, rounded, from_twin, halves, sending, from_row, leaving, arriving, part, folded, from_z, from_y, final, send, recv, near,
):
    y, z, c, x = position()
    links = Links(send, recv)
    x_peers = [device(y, z, c, (x + k) % NX) for k in range(1, NX)]
    z_peers = [device(y, (z + k) % NZ, c, x) for k in range(1, NZ)]
    y_peers = [device((y + k) % NY, z, c, x) for k in range(1, NY)]
    twin = device(y, z, 1 - c, x)
    z_far_first = [z_peers[k - 1] for k in FAR_FIRST]
    y_far_first = [y_peers[k - 1] for k in FAR_FIRST]
    x_up, x_down, z_up, z_down = x_peers[0], x_peers[-1], z_peers[0], z_peers[-1]
    y_up, y_down, y_up2, y_down2 = y_peers[0], y_peers[-1], y_peers[1], y_peers[-2]
    sent = []
    local = []

    def move(src, dst, target):
        made = links.copy(src, dst, target)
        sent.append(made)
        return made

    def push(ref, target):
        return move(ref, ref, target)

    def arrive(copies):
        for copy in copies:
            copy.wait_recv()

    def settle(leave):
        while len(sent) > leave:
            sent.pop(0).wait_send()

    def here(src, dst):
        made = pltpu.make_async_copy(src, dst, near.at[len(local)])
        made.start()
        local.append(made)
        return made

    barrier = pltpu.get_barrier_semaphore()
    peers = [peer for pair in zip(y_far_first, z_far_first) for peer in pair]
    peers += x_peers + [twin]
    for peer in peers:
        pl.semaphore_signal(barrier, inc=1, device_id=peer, device_id_type=MESH)
    load_feat = here(feat, held.at[0, z, x])
    load_sends = here(sends_in, sends)
    load_tiles = here(tiles_in, tiles)
    load_target = here(target_in, target)
    load_counts = here(counts_in, counts)
    load_hist = here(hist, held.at[1, z, x])
    mine = pl.ds(pl.multiple_of(x * ROWS, ROWS), ROWS)
    adj_here = adj.at[mine, :]
    later = [here(a, b) for a, b in ((adj_in, adj_here), (w1_in, w1), (w2_in, w2), (cot_in, cot))]

    top = pl.ds(0, FIRST)
    low = pl.ds(FIRST, ROWS - FIRST)
    low_first = pl.ds(FIRST, LAST_CUT - FIRST)
    low_last = pl.ds(LAST_CUT, ROWS - LAST_CUT)
    x_left, x_right = (x + NX - 1) % NX, (x + 1) % NX
    z_up2, z_down2 = z_peers[1], z_peers[-2]
    before2, after2 = (z + NZ - 2) % NZ, (z + 2) % NZ

    def gather(a):
        def low_x(steps):
            made = []
            for k in steps:
                at = held.at[a, (z + k) % NZ, x, low]
                made += [push(at, x_up), push(at, x_down)]
            return made

        def low_x_on(steps):
            made = []
            for k in steps:
                at = held.at[a, (z + k) % NZ]
                made += [push(at.at[x_left, low_first], x_up), push(at.at[x_right, low_last], x_down)]
            return made

        at = held.at[a, z, x, low]
        lz_far = [push(at, z_up2), push(at, z_down2)]
        tx = [push(held.at[a, z, x, top], peer) for peer in x_peers]
        lz_near = [push(at, z_up), push(at, z_down)]
        lx = {0: low_x([0])}
        ends = []
        yield
        arrive(tx)
        at = held.at[a, z, :, top]
        tz_far = [push(at, z_up2), push(at, z_down2)]
        tz_near = [push(at, z_up), push(at, z_down)]
        yield
        arrive(lz_far)
        up, down = held.at[a, before2, x], held.at[a, after2, x]
        lz_on = [push(up.at[low_first], z_up2), push(down.at[low_last], z_down2)]
        lz_on += [push(up.at[low], z_up), push(down.at[low], z_down)]
        lx[2] = low_x([2, 6])
        yield
        arrive(lz_near)
        lx[1] = low_x([1, 7])
        arrive(lx[0])
        ends += low_x_on([0])
        yield
        arrive(tz_far)
        up, down = held.at[a, before2], held.at[a, after2]
        tz_on = [
            push(up.at[pl.ds(0, NX // 2), top], z_up2),
            push(down.at[pl.ds(NX // 2, NX // 2), top], z_down2),
            push(up.at[:, top], z_up),
            push(down.at[:, top], z_down),
        ]
        yield
        arrive(lz_on)
        lx[3] = low_x([3, 5, 4])
        yield
        arrive(lx[2])
        ends += low_x_on([2, 6])
        arrive(lx[1])
        ends += low_x_on([1, 7])
        yield
        arrive(lx[3])
        ends += low_x_on([3, 5, 4])
        yield
        arrive(tz_near + tz_on + ends)
        yield

    gathers = gather(0), gather(1)

    def step(which):
        for letter in which:
            next(gathers["FH".index(letter)])

    span = NZ * NC * NX * CAP * RB
    n = iota((1, span), 1)
    place = ((n >> 5) & 7) * 64 + (((n >> 8) + c) & 1) * 32 + (n & 31)
    order = one_hot(iota((span, span), 0) == place)
    block = ((n >> 5) & 7) * 16 + (((n >> 8) + c) & 1) * 8 + ((n & 31) >> 2)
    block_order = one_hot(iota((ROWS, span), 0) == block)
    load_sends.wait()
    for k in range(NY):
        sb[z, x, k : k + 1, :] = sends[:, k * ROWS : (k + 1) * ROWS].astype(jnp.float32)
    load_target.wait()
    load_counts.wait()
    for k in range(NY):
        code[k : k + 1, :] = target[:, k * ROWS : (k + 1) * ROWS].astype(jnp.float32)
        used[k : k + 1, :] = counts[:, k * TILE : (k + 1) * TILE].astype(jnp.float32)
    pairs = one_hot(iota((TILE, ROWS), 0) == (iota((1, ROWS), 1) >> 1))
    usable = (iota((1, ROWS), 1) & 1).astype(jnp.float32) < dot(used[...].astype(jnp.bfloat16), pairs)
    marked = jnp.where(usable, code[...], -1.0).astype(jnp.bfloat16)
    codes[...] = dot(marked, block_order)
    load_tiles.wait()
    stacked = jnp.concatenate([tiles[:, k * span : (k + 1) * span] for k in range(NY)], axis=0)
    placed = dot(stacked, order).astype(jnp.bfloat16)
    for k in range(NY):
        values = placed[k * TILE : (k + 1) * TILE]
        marks = jnp.broadcast_to(codes[k : k + 1, :], (CODED - TILE, span)).astype(jnp.bfloat16)
        edges[c, k, 0:TILE, :] = values[:, :KEPT]
        edges[c, k, TILE:CODED, :] = marks[:, :KEPT]
        twin_edges[k, 0:TILE, :] = values[:, KEPT:]
        twin_edges[k, TILE:CODED, :] = marks[:, KEPT:]
    load_feat.wait()
    load_hist.wait()

    pl.semaphore_wait(barrier, len(peers))
    step("F")
    sb_x = [push(sb.at[z, x], peer) for peer in x_peers]
    across = move(twin_edges, edges.at[c], twin)
    arrive([across])
    seen[:, y] = edges[:, y]
    edge_copies = [
        move(edges.at[:, (y + k) % NY], seen.at[:, y], y_peers[k - 1]) for k in FAR_FIRST
    ]
    step("FFF")
    arrive(sb_x)
    sb_z = [push(sb.at[z], peer) for peer in z_far_first]
    step("HFHF")

    arrive(sb_z)
    r = iota((1, KEPT), 1)
    lane = ((z * NC + ((r >> 4) & 1)) * NX + x) * CAP + ((r >> 2) & 1)
    asked = dot(
        one_hot(iota((ROWS, KEPT), 0) == lane),
        sb[...].reshape(NZ * NX * NY, ROWS).astype(jnp.bfloat16),
        ((0,), (1,)),
    )
    r, i = iota((KEPT, KEPT), 0), iota((KEPT, KEPT), 1)
    fits = ((i & 7) == (r >> 5)) & (((i >> 3) & 1) == ((r >> 3) & 1))
    wanted = jnp.where(fits, asked, 0.0).astype(jnp.bfloat16)
    pair = one_hot((iota((KEPT, ROWS), 0) >> 4) == iota((KEPT, ROWS), 1))
    r = iota((KEPT, 1), 0)
    base = ((r >> 3) & 1) * ROWS + (r & 3)
    slots = dot(wanted, pair) * RB + base.astype(jnp.float32)
    lanes = iota((1, KEPT), 1).astype(jnp.float32)
    for q in range(16):
        chosen[q] = one_hot(slots[:, q : q + 1] == lanes)
    step("HFHFHF")

    def full_edges(core, k):
        values = seen[core, k, 0:TILE, :].astype(jnp.float32)
        mark = seen[core, k, TILE:CODED, :].astype(jnp.float32)[0:1, :]
        both = [jnp.where(mark == t, values, 0.0).astype(jnp.bfloat16) for t in range(ROWS // TILE)]
        return jnp.concatenate(both, axis=0)

    def partial_sums(a, between):
        def pick(q, carry):
            source = held[a, q // 2, pl.ds((q % 2) * 2, 2)].reshape(KEPT, WIDTH)
            value = dot(chosen[q], source).astype(jnp.bfloat16)
            blocks[:, pl.ds(pl.multiple_of(q * 16, 16), 16), :] = value.reshape(16, 16, WIDTH)
            return carry

        lax.fori_loop(0, 16, pick, 0, unroll=4)
        between()
        crossing = []
        for k in ORDER:
            to = (y + k) % NY
            for_twin[a, to] = dot(full_edges(1 - c, to), blocks[to * NC + 1 - c]).astype(jnp.bfloat16)
            crossing.append(move(for_twin.at[a, to], of_twin.at[a, to], twin))
        between()
        relayed, direct = [], []
        for k, copy in zip(ORDER, crossing):
            to = (y + k) % NY
            value = dot(full_edges(c, to), blocks[to * NC + c])
            arrive([copy])
            value += of_twin[a, to].astype(jnp.float32)
            if k == 0:
                got[a, 0] = value.astype(jnp.bfloat16)
                continue
            if k == 2 or k == 6:
                second_hop[a, k // 4] = value
                continue
            parts[a, k] = value.astype(jnp.bfloat16)
            if k == 4:
                for side, to_y in enumerate((y_up2, y_down2)):
                    at = pl.ds(side * HALF, HALF)
                    relayed.append(move(parts.at[a, k, at], relay4.at[a, side], to_y))
            elif k == 3 or k == 5:
                side = 0 if k == 3 else 1
                relayed.append(move(parts.at[a, k], relay3.at[a, side], (y_up, y_down)[side]))
            else:
                side = 0 if k == 1 else 1
                direct.append(move(parts.at[a, k], got.at[a, 1 + side], (y_up, y_down)[side]))

        def relay():
            arrive(relayed)
            for side, to_y in enumerate((y_up2, y_down2)):
                value = second_hop[a, side] + relay3[a, side].astype(jnp.float32)
                far = relay4[a, side].astype(jnp.float32)
                k = 2 if side == 0 else 6
                for at, add in ((0, side == 0), (HALF, side == 1)):
                    rows_of = value[at : at + HALF]
                    parts[a, k, at : at + HALF, :] = (rows_of + far if add else rows_of).astype(jnp.bfloat16)
                direct.append(move(parts.at[a, k], got.at[a, 3 + side], to_y))
            return direct

        return relay

    def near_sum(a, total, copies):
        arrive(copies[:2])
        for k in range(3):
            total += got[a, k].astype(jnp.float32)
        return total

    def halo_sum(a, total, copies):
        arrive(copies[2:])
        return total + (got[a, 3].astype(jnp.float32) + got[a, 4].astype(jnp.float32))

    arrive(edge_copies)

    relay_first = partial_sums(0, lambda: step("H"))
    for _ in gathers[1]:
        pass
    for copy in later:
        copy.wait()
    adj_copies = [push(adj_here, peer) for peer in x_peers]
    first_parts = relay_first()
    relay_second = partial_sums(1, lambda: None)

    def spread_rows(slot, value):
        rows[slot, mine, :] = value
        return [push(rows.at[slot, mine, :], peer) for peer in x_peers]

    inner1 = dot(adj[mine, :], held[0, z].reshape(NX * ROWS, WIDTH))
    sum1 = near_sum(0, inner1, first_parts)
    mixed1 = halo_sum(0, sum1, first_parts).astype(jnp.bfloat16)
    pre1 = dot(mixed1, w1[...])
    copies = spread_rows(0, (pre1 * sigmoid(pre1)).astype(jnp.bfloat16))
    second_parts = relay_second()
    results = [here(rows.at[0, mine, :], fresh_out)]
    slopes[x] = silu_slope(pre1).astype(jnp.bfloat16)
    turned[x] = mixed1.T
    settle(40)
    arrive(copies)
    row_copies = [push(ref.at[x], peer) for ref in (turned, slopes) for peer in x_peers]
    inner2 = dot(adj[mine, :], rows[0])
    w2_t[...] = w2[...].T
    sum2 = near_sum(1, inner2, second_parts)
    mixed2 = halo_sum(1, sum2, second_parts).astype(jnp.bfloat16)
    pre2 = dot(mixed2, w2[...])
    back2 = (cot[...].astype(jnp.float32) * silu_slope(pre2)).astype(jnp.bfloat16)
    upstream = dot(back2, w2_t[...]).astype(jnp.bfloat16)
    copies = spread_rows(1, upstream)

    half = WIDTH // NC
    piece = half // NX
    kept = pl.ds(pl.multiple_of(c * half, half), half)
    given = pl.ds(pl.multiple_of((1 - c) * half, half), half)

    def to_row(crossing):
        arrive([crossing])
        value = share[kept, :] + from_twin[...].astype(jnp.float32)
        halves[...] = value
        sending[...] = value.astype(jnp.bfloat16)
        made = []
        for k in (2, 1, 3):
            at = pl.ds(pl.multiple_of((x + k) % NX * piece, piece), piece)
            made.append(move(sending.at[at, :], from_row.at[k - 1], x_peers[k - 1]))
        return made

    share[...] = dot(mixed2, back2, ((0,), (0,)))
    rounded[...] = share[...].astype(jnp.bfloat16)
    crossing = move(rounded.at[given, :], from_twin, twin)
    layer[...] = (pre2 * sigmoid(pre2)).astype(jnp.bfloat16)
    results.append(here(layer, layer_out))
    shares = to_row(crossing)
    settle(8)
    arrive(shares)
    own = pl.ds(pl.multiple_of(x * piece, piece), piece)
    total = halves[own, :]
    for k in range(NX - 1):
        total += from_row[k].astype(jnp.float32)
    part[piece : 2 * piece, :] = total

    arrive(adj_copies)
    arrive(row_copies)
    arrive(copies)
    spread = dot(adj[...], rows[1])
    slope = slopes[...].reshape(NX * ROWS, WIDTH).astype(jnp.float32)
    back1 = (spread * slope).astype(jnp.bfloat16)

    def turned_rows(core):
        at = pl.ds(pl.multiple_of(core * half + x * piece, piece), piece)
        return jnp.concatenate([turned[k, at, :] for k in range(NX)], axis=1)

    first_grad = dot(jnp.concatenate([turned_rows(1 - c), turned_rows(c)], axis=0), back1)
    leaving[...] = first_grad[:piece].astype(jnp.bfloat16)
    arrive([move(leaving, arriving, twin)])
    part[0:piece, :] = first_grad[piece:] + arriving[...].astype(jnp.float32)
    small = 2 * piece // NZ
    lanes = WIDTH // 2

    def fold(value):
        return jnp.concatenate([value[:, :lanes], value[:, lanes:]], axis=0).astype(jnp.bfloat16)

    for k in range(NZ):
        folded[k] = fold(part[k * small : (k + 1) * small, :])
    copies = []
    for k in FAR_FIRST:
        copies.append(move(folded.at[(z + k) % NZ], from_z.at[k - 1], z_peers[k - 1]))
    settle(7)
    arrive(copies)
    total = folded[z].astype(jnp.float32)
    for k in range(NZ - 1):
        total += from_z[k].astype(jnp.float32)
    from_y[y] = total.astype(jnp.bfloat16)
    copies = [push(from_y.at[y], peer) for peer in y_far_first]
    settle(7)
    arrive(copies)
    total = from_y[0].astype(jnp.float32)
    for k in range(1, NY):
        total += from_y[k].astype(jnp.float32)
    final[c, x, z] = total.astype(jnp.bfloat16)
    copies = [push(final.at[c, x, z], peer) for peer in z_far_first]
    settle(7)
    arrive(copies)
    copies = [push(final.at[c, x], x_peers[k - 1]) for k in (2, 1, 3)]
    crossings = [push(final.at[c, x], twin)]
    settle(4)
    for k, copy in zip((2, 1, 3), copies):
        arrive([copy])
        crossings.append(push(final.at[c, (x + NX - k) % NX], twin))

    results.append(here(final.at[c], final_out.at[c]))
    arrive(crossings)
    results.append(here(final.at[1 - c], final_out.at[1 - c]))
    settle(0)
    for copy in results:
        copy.wait()


def keep_kernel(
    fresh_in, layer_in, final_in, fresh_out, layer_out, grad1, grad2, fresh, layer, final, grads, into, out
):
    pairs = ((final_in, final), (fresh_in, fresh), (layer_in, layer))
    loads = [pltpu.make_async_copy(src, dst, into.at[k]) for k, (src, dst) in enumerate(pairs)]
    pairs = ((grads.at[0], grad1), (grads.at[1], grad2), (fresh, fresh_out), (layer, layer_out))
    stores = [pltpu.make_async_copy(src, dst, out.at[k]) for k, (src, dst) in enumerate(pairs)]
    for load in loads:
        load.start()
    half, lanes = WIDTH // NC, WIDTH // 2
    piece = half // NX
    small = 2 * piece // NZ
    loads[0].wait()
    for which in range(2):
        for core in range(NC):
            for m in range(NX):
                for k in range(which * NZ // 2, (which + 1) * NZ // 2):
                    row = core * half + m * piece + k * small - which * piece
                    value = final[core, m, k].astype(jnp.float32)
                    grads[which, row : row + small, 0:lanes] = value[:small]
                    grads[which, row : row + small, lanes:WIDTH] = value[small:]
        stores[which].start()
    for load, store in zip(loads[1:], stores[2:]):
        load.wait()
        store.start()
    for store in stores:
        store.wait()


def per_device(*arguments):
    f32, bf16, i32 = jnp.float32, jnp.bfloat16, jnp.int32
    piece = WIDTH // (NX * NC)
    span = NZ * NC * NX * CAP * RB
    n_copies = 210
    anywhere = pl.BlockSpec(memory_space=pl.ANY)
    shapes = (
        jax.ShapeDtypeStruct((ROWS, WIDTH), bf16),
        jax.ShapeDtypeStruct((ROWS, WIDTH), bf16),
        jax.ShapeDtypeStruct((WIDTH, WIDTH), f32),
        jax.ShapeDtypeStruct((WIDTH, WIDTH), f32),
    )
    packed = jax.ShapeDtypeStruct((NC, NX, NZ, 4 * piece // NZ, WIDTH // 2), bf16)
    results = pl.pallas_call(
        kernel,
        out_shape=shapes[:2] + (packed,),
        in_specs=[anywhere] * 10,
        out_specs=(anywhere,) * 3,
        scratch_shapes=[
            pltpu.VMEM((NX * ROWS, NX * ROWS), bf16),
            pltpu.VMEM((TILE, NY * span), bf16),
            pltpu.VMEM((1, NY * ROWS), i32),
            pltpu.VMEM((1, NY * TILE), i32),
            pltpu.VMEM((1, NY * ROWS), i32),
            pltpu.VMEM((WIDTH, WIDTH), bf16),
            pltpu.VMEM((WIDTH, WIDTH), bf16),
            pltpu.VMEM((WIDTH, WIDTH), bf16),
            pltpu.VMEM((ROWS, WIDTH), bf16),
            pltpu.VMEM((ROWS, WIDTH), bf16),
            pltpu.VMEM((2, NZ, NX, ROWS, WIDTH), bf16),
            pltpu.VMEM((NZ, NX, NY, ROWS), f32),
            pltpu.VMEM((NY, ROWS), f32),
            pltpu.VMEM((NY, TILE), f32),
            pltpu.VMEM((16, KEPT, KEPT), bf16),
            pltpu.VMEM((NY, span), f32),
            pltpu.VMEM((NC, NY, CODED, KEPT), bf16),
            pltpu.VMEM((NY, CODED, KEPT), bf16),
            pltpu.VMEM((NC, NY, CODED, KEPT), bf16),
            pltpu.VMEM((NY * NC, KEPT, WIDTH), bf16),
            pltpu.VMEM((2, NY, ROWS, WIDTH), bf16),
            pltpu.VMEM((2, NY, ROWS, WIDTH), bf16),
            pltpu.VMEM((2, NY, ROWS, WIDTH), bf16),
            pltpu.VMEM((2, 2, ROWS, WIDTH), f32),
            pltpu.VMEM((2, 2, ROWS, WIDTH), bf16),
            pltpu.VMEM((2, 2, HALF, WIDTH), bf16),
            pltpu.VMEM((2, 5, ROWS, WIDTH), bf16),
            pltpu.VMEM((2, NX * ROWS, WIDTH), bf16),
            pltpu.VMEM((NX, ROWS, WIDTH), bf16),
            pltpu.VMEM((NX, WIDTH, ROWS), bf16),
            pltpu.VMEM((WIDTH, WIDTH), f32),
            pltpu.VMEM((WIDTH, WIDTH), bf16),
            pltpu.VMEM((WIDTH // NC, WIDTH), bf16),
            pltpu.VMEM((WIDTH // NC, WIDTH), f32),
            pltpu.VMEM((WIDTH // NC, WIDTH), bf16),
            pltpu.VMEM((NX - 1, piece, WIDTH), bf16),
            pltpu.VMEM((piece, WIDTH), bf16),
            pltpu.VMEM((piece, WIDTH), bf16),
            pltpu.VMEM((2 * piece, WIDTH), f32),
            pltpu.VMEM((NZ, 4 * piece // NZ, WIDTH // 2), bf16),
            pltpu.VMEM((NZ - 1, 4 * piece // NZ, WIDTH // 2), bf16),
            pltpu.VMEM((NY, 4 * piece // NZ, WIDTH // 2), bf16),
            pltpu.VMEM((NC, NX, NZ, 4 * piece // NZ, WIDTH // 2), bf16),
            pltpu.SemaphoreType.DMA((n_copies,)),
            pltpu.SemaphoreType.DMA((n_copies,)),
            pltpu.SemaphoreType.DMA((16,)),
        ],
        compiler_params=pltpu.CompilerParams(
            collective_id=0, has_side_effects=True, vmem_limit_bytes=56 * 1024 * 1024
        ),
        name="layers",
    )(*arguments)
    return pl.pallas_call(
        keep_kernel,
        out_shape=shapes,
        in_specs=[anywhere] * 3,
        out_specs=(anywhere,) * 4,
        scratch_shapes=[pltpu.VMEM(shape.shape, shape.dtype) for shape in shapes[:2] + (packed,)]
        + [pltpu.VMEM((2, WIDTH, WIDTH), f32)]
        + [pltpu.SemaphoreType.DMA((3,)), pltpu.SemaphoreType.DMA((4,))],
        compiler_params=pltpu.CompilerParams(vmem_limit_bytes=60 * 1024 * 1024),
        name="keep",
    )(*results)


def solution(mesh):
    spread = P(("dom", "row"), None)
    in_specs = (spread,) * 7 + (P(), P(), spread)
    out_specs = (spread, spread, P(), P())
    return jax.shard_map(
        per_device, mesh=mesh, in_specs=in_specs, out_specs=out_specs, check_vma=False
    )
```
